256 devices in a mesh: tp: 16 (over z, x_hi), sp: 16 (over y, x_lo, core).
Axes of the slice: x: 4 (x_hi: 2, x_lo: 2; x = x_hi * 2 + x_lo), y: 4, z: 8, core: 2. Of those that a mesh axis runs over, the one named last changes fastest.
Arguments:
- context: bfloat16 [2048, 16384], P('sp', 'tp'), may hold values from -6 to 6
- w_out: bfloat16 [16384, 16384], P('tp', 'sp'), may hold values from -0.046875 to 0.046875
- teacher_resid: bfloat16 [2048, 16384], P('tp', 'sp'), may hold values from -3 to 3
- queries: bfloat16 [2048, 4096], P('sp', 'tp'), may hold values from -5 to 5
- keys: bfloat16 [2048, 4096], P('sp', 'tp'), may hold values from -5 to 5
- values: bfloat16 [2048, 4096], P('sp', 'tp'), may hold values from -6 to 6
- segment_ids: int32 [2048], replicated, may hold values from 0 to 3, never falling along the last dimension, each value on 1 to 1024 neighbouring positions
- proj: bfloat16 [4096, 16384], P('tp', 'sp'), may hold values from -0.75 to 0.75
Outputs:
- proj_grad: bfloat16 [4096, 16384], P('tp', 'sp')
- query_grad: bfloat16 [2048, 4096], P('sp', 'tp')
- key_grad: bfloat16 [2048, 4096], P('sp', 'tp')
- value_grad: bfloat16 [2048, 4096], P('sp', 'tp')
The draws below stay inside these ranges and needn't reach their ends.
All inputs are finite; a program needn't handle non-finite values.
Results may differ from the reference program's by a relative error of at most 0.02.
Values may be sent and summed in bfloat16 or wider, within the bound.
No kernel may reach another device: no remote copies, remote signals or barrier semaphores. Data moves between devices by JAX's collectives and lax.ppermute only.
A program may use at most 128 MiB of HBM per device.

```python
import math
import jax
import jax.numpy as jnp
import numpy as np
from jax import lax

DT = 16384
HEADS = 32
HEAD_DIM = 128
TOK_DEV = 128
DS = 4096
PACKED_TOKENS = 2048
N_SP = 16


def draw_queries(key, part):
    key = jax.random.fold_in(key, 1)
    base = jnp.clip(1.5 * jax.random.normal(key, (PACKED_TOKENS, DS), jnp.float32), -5.0, 5.0)
    return base.astype(jnp.bfloat16)


def draw_keys(key, part):
    key = jax.random.fold_in(key, 2)
    base = jnp.clip(1.5 * jax.random.normal(key, (PACKED_TOKENS, DS), jnp.float32), -5.0, 5.0)
    return base.astype(jnp.bfloat16)


def spiked(result, own_key, source, target, shards_of, factor):
    owner, partner = [(jnp.arange(result.shape[dim]) // (result.shape[dim] // shards_of)).reshape([-1 if axis == dim else 1 for axis in range(result.ndim)]) for dim in (source, target)]
    chosen = jax.random.permutation(own_key, shards_of)[partner]
    strong = (owner == chosen) | (owner == (partner + shards_of // 2) % shards_of)
    return jnp.where(strong, factor * result, result)


def steps_of(rng, extent, pieces, least, top_value):
    factor_of = 1.0
    for dim, shards_of in pieces:
        draws = jax.random.uniform(jax.random.fold_in(jax.random.fold_in(rng, 6), dim), (shards_of,), jnp.float32, least / len(pieces), top_value / len(pieces))
        factor_of = factor_of * jnp.repeat(jnp.exp(draws), extent[dim] // shards_of).reshape((-1,) + (1,) * (len(extent) - 1 - dim))
    return factor_of


def profile(amount, total, bound, lean):
    loads = [(1 << 20) // math.isqrt(grade ** lean) + 1 for grade in range(2, amount + 1)]
    spare, counts = total - bound - (amount - 1), [1] * (amount - 1)
    while spare > 0:
        candidates = [i for i in range(amount - 1) if counts[i] < bound]
        whole, left = sum([loads[i] for i in candidates]), spare
        for i in candidates:
            extra = min(bound - counts[i], max(1, left * loads[i] // whole), spare)
            counts[i] = counts[i] + extra
            spare = spare - extra
    return np.array([bound] + counts)


def ragged_sizes(own_key, count, total, limit, skew):
    if count == 2:
        one = jax.random.randint(own_key, (), max(1, total - limit), min(limit, total - 1) + 1)
        return jnp.stack([one, total - one])
    tallies = jnp.asarray(profile(count, total, limit, skew), jnp.int32)
    pairs = (count - 1) // 2
    source_of, taker = tallies[1:1 + 2 * pairs:2], tallies[2:2 + 2 * pairs:2]
    margin = jnp.minimum(source_of - 1, limit - taker)
    passed = jax.random.randint(jax.random.fold_in(own_key, 1), (pairs,), 0, 1 << 20) % (margin + 1)
    tallies = tallies.at[1:1 + 2 * pairs:2].set(source_of - passed).at[2:2 + 2 * pairs:2].set(taker + passed)
    return tallies[jax.random.permutation(jax.random.fold_in(own_key, 2), count)]


def bell_draw(own_key, shape, scale, reach, shards=(), kind=jnp.bfloat16):
    gain = steps_of(own_key, shape, shards, -0.22, 0.18) if shards else 1.0
    array = jax.random.normal(own_key, shape, jnp.float32) * scale * gain
    return jnp.minimum(jnp.maximum(array, -reach), reach).astype(kind)


def bell_draw_with(key, extent, width, reach, cuts, heavy, kind=jnp.bfloat16):
    entries = width * jax.random.normal(key, extent, jnp.float32)
    if cuts:
        entries = entries * steps_of(key, extent, cuts, -0.22, 0.18)
    return jnp.clip(spiked(entries, jax.random.fold_in(key, 3), *heavy), -reach, reach).astype(kind)


def setup_inputs(seed: int = 0) -> dict:
    arg_keys = jax.random.split(jax.random.key(seed), 9)
    context = bell_draw_with(arg_keys[0], (PACKED_TOKENS, DT), 1.0, 6.0, ((0, 16), (1, 16)), (1, 0, 16, 2.0))
    w_out = bell_draw(arg_keys[1], (DT, DT), DT ** -0.5, 0.046875, ((0, 16), (1, 16)))
    teacher_resid = bell_draw(arg_keys[2], (PACKED_TOKENS, DT), 0.5, 3.0, ((0, 16), (1, 16)))
    queries = draw_queries(jax.random.fold_in(arg_keys[8], 71), 0)
    keys = draw_keys(jax.random.fold_in(arg_keys[8], 71), 0)
    values = bell_draw(arg_keys[5], (PACKED_TOKENS, DS), 1.0, 6.0, ((0, 16), (1, 16)))
    segment_ids = jnp.searchsorted(jnp.cumsum(ragged_sizes(arg_keys[6], max(3, PACKED_TOKENS // 512), PACKED_TOKENS, PACKED_TOKENS // 2, 0)), jnp.arange(PACKED_TOKENS), side="right").astype(jnp.int32)
    proj = bell_draw(arg_keys[7], (DS, DT), (DS // 64) ** -0.5, 0.75, ((0, 16), (1, 16)))
    return {"context": context, "w_out": w_out, "teacher_resid": teacher_resid, "queries": queries, "keys": keys, "values": values, "segment_ids": segment_ids, "proj": proj}


def head_forward(query_h, key_h, value_h, allowed):
    scale = HEAD_DIM ** -0.5
    scores = jnp.dot(query_h, key_h.T, preferred_element_type=jnp.float32) * scale
    scores = jnp.where(allowed, scores, -1e30)
    top = jnp.max(scores, axis=-1, keepdims=True)
    expo = jnp.exp(scores - top)
    probs = expo / jnp.sum(expo, axis=-1, keepdims=True)
    probs_low = probs.astype(jnp.bfloat16)
    return probs, probs_low


def reference(context, w_out, teacher_resid, queries, keys, values, segment_ids, proj):
    scale = HEAD_DIM ** -0.5
    distill_target = teacher_resid.astype(jnp.float32) + jnp.dot(context, w_out, preferred_element_type=jnp.float32)
    places = jnp.arange(PACKED_TOKENS, dtype=jnp.int32)
    allowed = (places[:, None] >= places[None, :]) & (segment_ids[:, None] == segment_ids[None, :])
    query_heads = queries.reshape(PACKED_TOKENS, HEADS, HEAD_DIM).transpose(1, 0, 2)
    key_heads = keys.reshape(PACKED_TOKENS, HEADS, HEAD_DIM).transpose(1, 0, 2)
    value_heads = values.reshape(PACKED_TOKENS, HEADS, HEAD_DIM).transpose(1, 0, 2)

    def forward_one(items):
        query_h, key_h, value_h = items
        probs, probs_low = head_forward(query_h, key_h, value_h, allowed)
        return jnp.dot(probs_low, value_h, preferred_element_type=jnp.float32).astype(jnp.bfloat16)

    attention_per_head = lax.map(forward_one, (query_heads, key_heads, value_heads))
    attn = attention_per_head.transpose(1, 0, 2).reshape(PACKED_TOKENS, DS)
    pred = jnp.dot(attn, proj, preferred_element_type=jnp.float32)
    diff = pred - distill_target
    dpred = diff.astype(jnp.bfloat16)
    proj_grad = jnp.dot(attn.T, dpred, preferred_element_type=jnp.float32).astype(jnp.bfloat16)
    dattn = jnp.dot(dpred, proj.T, preferred_element_type=jnp.float32).astype(jnp.bfloat16)
    dattn_heads = dattn.reshape(PACKED_TOKENS, HEADS, HEAD_DIM).transpose(1, 0, 2)

    def block_sum(left, right):
        leading_blocks = left.reshape(N_SP, TOK_DEV, PACKED_TOKENS).astype(jnp.float32)
        trailing_blocks = right.reshape(N_SP, TOK_DEV, HEAD_DIM).astype(jnp.float32)
        split_pieces = jnp.einsum('iep,ieg->ipg', leading_blocks, trailing_blocks).astype(jnp.bfloat16)
        split_pieces = lax.optimization_barrier(split_pieces)
        return jnp.sum(split_pieces.astype(jnp.float32), axis=0).astype(jnp.bfloat16)

    def backward_one(items):
        query_h, key_h, value_h, attn_h, dattn_h = items
        probs, probs_low = head_forward(query_h, key_h, value_h, allowed)
        delta = jnp.sum(dattn_h.astype(jnp.float32) * attn_h.astype(jnp.float32), axis=-1)
        dprobs = jnp.dot(dattn_h, value_h.T, preferred_element_type=jnp.float32)
        dscores = (probs * (dprobs - delta[:, None]) * scale).astype(jnp.bfloat16)
        query_g = jnp.dot(dscores, key_h, preferred_element_type=jnp.float32).astype(jnp.bfloat16)
        key_g = block_sum(dscores, query_h)
        value_g = block_sum(probs_low, dattn_h)
        return query_g, key_g, value_g

    query_g, key_g, value_g = lax.map(backward_one, (query_heads, key_heads, value_heads, attention_per_head, dattn_heads))

    def merge_heads(grads):
        return grads.transpose(1, 0, 2).reshape(PACKED_TOKENS, DS)

    return proj_grad, merge_heads(query_g), merge_heads(key_g), merge_heads(value_g)
```

```python
import functools

import jax
import jax.numpy as jnp
from jax import lax
from jax.experimental import pallas as pl
from jax.experimental.pallas import tpu as pltpu
from jax.sharding import Mesh
from jax.sharding import PartitionSpec as P

HEAD_DIM = 128
SEGMENT_MAX = 1024
TP = ("z", "xh")
SP = ("y", "xl", "core")
F32 = jnp.float32
BF16 = jnp.bfloat16
NT = (((1,), (1,)), ((), ()))
TN = (((0,), (0,)), ((), ()))


def dot(a, b, dims=(((1,), (0,)), ((), ()))):
    return lax.dot_general(a, b, dims, preferred_element_type=F32)


def forward_kernel(q_ref, qseg_ref, kseg_ref, *refs):
    kv_refs, (attn_ref, probs_ref) = refs[:-2], refs[-2:]
    rows, width = q_ref.shape
    keys = rows * len(kv_refs)
    scale = HEAD_DIM ** (-0.5)
    place = lax.broadcasted_iota(jnp.int32, (rows, keys), 0) + (keys - rows)
    allowed = (place >= lax.broadcasted_iota(jnp.int32, (rows, keys), 1)) & (
        qseg_ref[...] == kseg_ref[...]
    )
    for h in range(width // HEAD_DIM):
        cols = slice(h * HEAD_DIM, (h + 1) * HEAD_DIM)
        vcols = slice(width + h * HEAD_DIM, width + (h + 1) * HEAD_DIM)
        key = jnp.concatenate([r[:, cols] for r in kv_refs], axis=0)
        value = jnp.concatenate([r[:, vcols] for r in kv_refs], axis=0)
        scores = jnp.where(allowed, dot(q_ref[:, cols], key, NT) * scale, -1e30)
        expo = jnp.exp(scores - jnp.max(scores, axis=-1, keepdims=True))
        probs = expo / jnp.sum(expo, axis=-1, keepdims=True)
        probs_ref[h] = probs
        attn_ref[:, cols] = dot(probs.astype(BF16), value).astype(BF16)


def backward_kernel(q_ref, attn_ref, dattn_ref, probs_ref, *refs):
    n = (len(refs) - 1) // 2
    kv_refs, dq_ref, dkv_refs = refs[:n], refs[n], refs[n + 1 :]
    rows, width = q_ref.shape
    scale = HEAD_DIM ** (-0.5)
    for h in range(width // HEAD_DIM):
        cols = slice(h * HEAD_DIM, (h + 1) * HEAD_DIM)
        vcols = slice(width + h * HEAD_DIM, width + (h + 1) * HEAD_DIM)
        key = jnp.concatenate([r[:, cols] for r in kv_refs], axis=0)
        value = jnp.concatenate([r[:, vcols] for r in kv_refs], axis=0)
        probs = probs_ref[h]
        dattn = dattn_ref[:, cols]
        delta = jnp.sum(
            dattn.astype(F32) * attn_ref[:, cols].astype(F32), axis=-1, keepdims=True
        )
        dprobs = dot(dattn, value, NT)
        dscores = (probs * (dprobs - delta) * scale).astype(BF16)
        dq_ref[:, cols] = dot(dscores, key).astype(BF16)
        dkey = dot(dscores, q_ref[:, cols], TN).astype(BF16)
        dvalue = dot(probs.astype(BF16), dattn, TN).astype(BF16)
        for i, r in enumerate(dkv_refs):
            r[:, cols] = dkey[i * rows : (i + 1) * rows]
            r[:, vcols] = dvalue[i * rows : (i + 1) * rows]


def call(kernel, out_shape, *args):
    return pl.pallas_call(
        kernel,
        out_shape=out_shape,
        compiler_params=pltpu.CompilerParams(vmem_limit_bytes=40 * 1024 * 1024),
    )(*args)


def body(context, w_out, teacher_resid, queries, keys, values, segment_ids, proj):
    rows, width = queries.shape
    heads = width // HEAD_DIM
    n_sp = lax.axis_size(SP)
    n_xh = lax.axis_size("xh")
    back = -(-(SEGMENT_MAX - 1) // rows)
    back = min(back, n_sp - 1)
    window = (back + 1) * rows
    me = lax.axis_index(SP)
    first_row = me * rows

    def shift(array, by):
        pairs = [(i, i + by) for i in range(n_sp) if 0 <= i + by < n_sp]
        return lax.ppermute(array, SP, pairs)

    def swap(array):
        return lax.ppermute(array, "xh", [(i, i ^ 1) for i in range(n_xh)])

    context_all = lax.all_gather(context, SP, axis=0, tiled=True)

    key_value = jnp.concatenate([keys, values], axis=1)
    blocks = [shift(key_value, k) for k in range(back, 0, -1)] + [key_value]
    padded = jnp.concatenate([jnp.full((window - rows,), -1, jnp.int32), segment_ids])
    window_segments = lax.dynamic_slice_in_dim(padded, first_row, window, 0)
    query_segments = lax.dynamic_slice_in_dim(segment_ids, first_row, rows, 0)
    attn, probs = call(
        forward_kernel,
        (
            jax.ShapeDtypeStruct((rows, width), BF16),
            jax.ShapeDtypeStruct((heads, rows, window), F32),
        ),
        queries,
        query_segments[:, None],
        window_segments[None, :],
        *blocks,
    )
    attn_all = lax.all_to_all(
        jnp.broadcast_to(attn[None], (n_sp, rows, width)), SP, 0, 0, tiled=True
    ).reshape(n_sp * rows, width)

    part = (dot(attn_all, proj) - dot(context_all, w_out)).astype(BF16)
    part = lax.psum_scatter(part, "z", scatter_dimension=0, tiled=True)
    xh = lax.axis_index("xh")
    mine = lax.dynamic_slice_in_dim(part, xh * rows, rows, 0)
    other = lax.dynamic_slice_in_dim(part, (1 - xh) * rows, rows, 0)
    diff = mine.astype(F32) + swap(other).astype(F32) - teacher_resid.astype(F32)
    dpred = diff.astype(BF16)

    theirs = swap(dpred)
    pair = jnp.concatenate(
        [jnp.where(xh == 0, dpred, theirs), jnp.where(xh == 0, theirs, dpred)], axis=0
    )
    dpred_all = lax.all_gather(pair, "z", axis=0, tiled=True)

    dattn_part = dot(dpred_all, proj, NT).astype(BF16).reshape(n_sp, rows, width)
    dattn_parts = lax.all_to_all(dattn_part, SP, 0, 0, tiled=True)
    dattn = jnp.sum(dattn_parts.astype(F32), axis=0).astype(BF16)
    proj_grad = dot(attn_all, dpred_all, TN).astype(BF16)

    query_grad, *grads = call(
        backward_kernel,
        (jax.ShapeDtypeStruct((rows, width), BF16),)
        + (jax.ShapeDtypeStruct((rows, 2 * width), BF16),) * (back + 1),
        queries,
        attn,
        dattn,
        probs,
        *blocks,
    )
    total = grads[back].astype(F32)
    for k in range(1, back + 1):
        total = total + shift(grads[back - k], -k).astype(F32)
    total = total.astype(BF16)
    return proj_grad, query_grad, total[:, :width], total[:, width:]


def solution(mesh):
    fine = Mesh(mesh.devices.reshape(8, 2, 4, 2, 2), TP + SP)
    in_specs = (
        P(SP, TP),
        P(TP, SP),
        P(TP, SP),
        P(SP, TP),
        P(SP, TP),
        P(SP, TP),
        P(),
        P(TP, SP),
    )
    out_specs = (P(TP, SP), P(SP, TP), P(SP, TP), P(SP, TP))
    return jax.shard_map(body, mesh=fine, in_specs=in_specs, out_specs=out_specs, check_vma=False)
```

```python
import functools

import jax
import jax.numpy as jnp
from jax import lax
from jax.experimental import pallas as pl
from jax.experimental.pallas import tpu as pltpu
from jax.sharding import Mesh
from jax.sharding import PartitionSpec as P

HEAD_DIM = 128
SEGMENT_MAX = 1024
TP = ("z", "xh")
SP = ("y", "xl", "core")
F32 = jnp.float32
BF16 = jnp.bfloat16
NT = (((1,), (1,)), ((), ()))
TN = (((0,), (0,)), ((), ()))


def dot(a, b, dims=(((1,), (0,)), ((), ()))):
    return lax.dot_general(a, b, dims, preferred_element_type=F32)


def fetch(sources, targets, sems):
    copies = [
        pltpu.make_async_copy(src, dst, sems.at[i])
        for i, (src, dst) in enumerate(zip(sources, targets, strict=True))
    ]
    for copy in copies:
        copy.start()
    for copy in copies:
        copy.wait()


def forward_kernel(n, qseg_ref, kseg_ref, q_hbm, *refs):
    kv_hbm, (attn_ref, probs_ref, q_ref, kv_ref, sems) = refs[:n], refs[n:]
    rows, width = q_ref.shape
    keys = rows * n
    fetch(
        (q_hbm, *kv_hbm),
        (q_ref, *(kv_ref.at[pl.ds(i * rows, rows)] for i in range(n))),
        sems,
    )
    scale = HEAD_DIM ** (-0.5)
    place = lax.broadcasted_iota(jnp.int32, (rows, keys), 0) + (keys - rows)
    allowed = (place >= lax.broadcasted_iota(jnp.int32, (rows, keys), 1)) & (
        qseg_ref[...] == kseg_ref[...]
    )
    for h in range(width // HEAD_DIM):
        cols = slice(h * HEAD_DIM, (h + 1) * HEAD_DIM)
        vcols = slice(width + h * HEAD_DIM, width + (h + 1) * HEAD_DIM)
        scores = jnp.where(allowed, dot(q_ref[:, cols], kv_ref[:, cols], NT) * scale, -1e30)
        expo = jnp.exp(scores - jnp.max(scores, axis=-1, keepdims=True))
        probs = expo / jnp.sum(expo, axis=-1, keepdims=True)
        probs_ref[h] = probs
        attn_ref[:, cols] = dot(probs.astype(BF16), kv_ref[:, vcols]).astype(BF16)


def backward_kernel(n, dattn_ref, q_hbm, attn_hbm, probs_hbm, *refs):
    kv_hbm, dq_ref, dkv_refs = refs[:n], refs[n], refs[n + 1 : 2 * n + 1]
    q_ref, attn_ref, probs_ref, kv_ref, sems = refs[2 * n + 1 :]
    rows, width = q_ref.shape
    fetch(
        (q_hbm, attn_hbm, probs_hbm, *kv_hbm),
        (q_ref, attn_ref, probs_ref, *(kv_ref.at[pl.ds(i * rows, rows)] for i in range(n))),
        sems,
    )
    scale = HEAD_DIM ** (-0.5)
    for h in range(width // HEAD_DIM):
        cols = slice(h * HEAD_DIM, (h + 1) * HEAD_DIM)
        vcols = slice(width + h * HEAD_DIM, width + (h + 1) * HEAD_DIM)
        probs = probs_ref[h]
        dattn = dattn_ref[:, cols]
        delta = jnp.sum(
            dattn.astype(F32) * attn_ref[:, cols].astype(F32), axis=-1, keepdims=True
        )
        dprobs = dot(dattn, kv_ref[:, vcols], NT)
        dscores = (probs * (dprobs - delta) * scale).astype(BF16)
        dq_ref[:, cols] = dot(dscores, kv_ref[:, cols]).astype(BF16)
        dkey = dot(dscores, q_ref[:, cols], TN).astype(BF16)
        dvalue = dot(probs.astype(BF16), dattn, TN).astype(BF16)
        for i, r in enumerate(dkv_refs):
            r[:, cols] = dkey[i * rows : (i + 1) * rows]
            r[:, vcols] = dvalue[i * rows : (i + 1) * rows]


def dattn_kernel(n, offsets, z_ref, dpred_ref, *refs):
    proj_hbm, (out_ref, *proj_refs, sems) = refs[: len(offsets)], refs[len(offsets) :]
    fetch(proj_hbm, proj_refs, sems)
    first = [0] * n
    for ref, by in zip(proj_refs, offsets, strict=True):
        size = ref.shape[0]
        z = lax.rem(z_ref[0] + by, n)
        out = dot(dpred_ref[...], ref[...], NT).astype(BF16)
        out_ref[z, :, first[by] : first[by] + size] = out
        first[by] += size


def call(kernel, out_shape, in_vmem, in_hbm, scratch, scalars=()):
    return pl.pallas_call(
        kernel,
        out_shape=out_shape,
        in_specs=[pl.BlockSpec(memory_space=pltpu.SMEM)] * len(scalars)
        + [pl.BlockSpec(memory_space=pltpu.VMEM)] * len(in_vmem)
        + [pl.BlockSpec(memory_space=pl.ANY)] * len(in_hbm),
        scratch_shapes=[pltpu.VMEM(s.shape, s.dtype) for s in scratch]
        + [pltpu.SemaphoreType.DMA((len(in_hbm),))],
        compiler_params=pltpu.CompilerParams(vmem_limit_bytes=40 * 1024 * 1024),
    )(*scalars, *in_vmem, *in_hbm)


def body(context, w_out, teacher_resid, queries, keys, values, segment_ids, proj):
    rows, width = queries.shape
    heads = width // HEAD_DIM
    n_sp, n_z, n_xh = lax.axis_size(SP), lax.axis_size("z"), lax.axis_size("xh")
    back = -(-(SEGMENT_MAX - 1) // rows)
    back = min(back, n_sp - 1)
    window = (back + 1) * rows
    first_row = lax.axis_index(SP) * rows
    z, xh = lax.axis_index("z"), lax.axis_index("xh")

    def shift(array, by):
        pairs = [(i, i + by) for i in range(n_sp) if 0 <= i + by < n_sp]
        return lax.ppermute(array, SP, pairs)

    def turn(array, by):
        return lax.ppermute(array, "z", [(i, (i + by) % n_z) for i in range(n_z)])

    def swap(array):
        return lax.ppermute(array, "xh", [(i, i ^ 1) for i in range(n_xh)])

    context_all = lax.all_gather(context, SP, axis=0, tiled=True)

    half = width // 2
    pieces, offsets = [proj], [0]

    def step(up, down):
        k = len(pieces) // 2 + 1
        if k == n_z // 2:
            up, down = up[:half], down[half:]
        offsets.extend([n_z - k, k])
        return turn(up, 1), turn(down, -1)

    key_value = jnp.concatenate([keys, values], axis=1)
    blocks = [shift(key_value, k) for k in range(back, 0, -1)] + [key_value]
    padded = jnp.concatenate([jnp.full((window - rows,), -1, jnp.int32), segment_ids])
    window_segments = lax.dynamic_slice_in_dim(padded, first_row, window, 0)
    query_segments = lax.dynamic_slice_in_dim(segment_ids, first_row, rows, 0)
    block_type = jax.ShapeDtypeStruct((rows, width), BF16)
    window_type = jax.ShapeDtypeStruct((window, 2 * width), BF16)
    probs_type = jax.ShapeDtypeStruct((heads, rows, window), F32)
    up, down = step(proj, proj)
    queries, up, down = lax.optimization_barrier((queries, up, down))
    pieces += [up, down]
    attn, probs = call(
        functools.partial(forward_kernel, back + 1),
        (block_type, probs_type),
        (query_segments[:, None], window_segments[None, :]),
        (queries, *blocks),
        (block_type, window_type),
    )
    attn_all = lax.all_to_all(
        jnp.broadcast_to(attn[None], (n_sp, rows, width)), SP, 0, 0, tiled=True
    ).reshape(n_sp * rows, width)
    up, down = step(up, down)
    attn_all, up, down = lax.optimization_barrier((attn_all, up, down))
    pieces += [up, down]

    resid_other = swap(teacher_resid)
    resid = jnp.concatenate(
        [
            jnp.where(xh == 0, teacher_resid, resid_other),
            jnp.where(xh == 0, resid_other, teacher_resid),
        ],
        axis=0,
    )
    part = (dot(attn_all, proj) - dot(context_all, w_out)).astype(BF16)
    part = lax.psum_scatter(part, "z", scatter_dimension=0, tiled=True)
    while len(pieces) < n_z:
        up, down = step(up, down)
        pieces += [up, down]
    part, resid, up, down = lax.optimization_barrier((part, resid, up, down))
    pieces[-2:] = [up, down]
    diff = (part.astype(F32) + swap(part).astype(F32)) - resid.astype(F32)
    dpred = diff.astype(BF16)

    dattn_part = call(
        functools.partial(dattn_kernel, n_z, offsets),
        jax.ShapeDtypeStruct((n_z, n_xh * rows, width), BF16),
        (dpred,),
        pieces,
        pieces,
        scalars=(z[None],),
    )
    dattn_parts = lax.all_to_all(dattn_part.reshape(n_sp, rows, width), SP, 0, 0, tiled=True)
    dattn = jnp.sum(dattn_parts.astype(F32), axis=0).astype(BF16)
    pairs = []
    for a in range(n_z):
        for x in range(n_xh):
            for b in range(n_z):
                for e in range(n_xh):
                    pairs.append(
                        (
                            (a * n_xh + x) * n_sp + b * n_xh + e,
                            (b * n_xh + x) * n_sp + a * n_xh + e,
                        )
                    )
    dattn = lax.ppermute(dattn, TP + SP, pairs)

    dpred_all = lax.all_gather(dpred, "z", axis=0, tiled=True)
    proj_grad = dot(attn_all, dpred_all, TN).astype(BF16)

    query_grad, *grads = call(
        functools.partial(backward_kernel, back + 1),
        (block_type,) + (jax.ShapeDtypeStruct((rows, 2 * width), BF16),) * (back + 1),
        (dattn,),
        (queries, attn, probs, *blocks),
        (block_type, block_type, probs_type, window_type),
    )
    total = grads[back].astype(F32)
    for k in range(1, back + 1):
        total = total + shift(grads[back - k], -k).astype(F32)
    total = total.astype(BF16)
    return proj_grad, query_grad, total[:, :width], total[:, width:]


def solution(mesh):
    fine = Mesh(mesh.devices.reshape(8, 2, 4, 2, 2), TP + SP)
    in_specs = (
        P(SP, TP),
        P(TP, SP),
        P(TP, SP),
        P(SP, TP),
        P(SP, TP),
        P(SP, TP),
        P(),
        P(TP, SP),
    )
    out_specs = (P(TP, SP), P(SP, TP), P(SP, TP), P(SP, TP))
    return jax.shard_map(body, mesh=fine, in_specs=in_specs, out_specs=out_specs, check_vma=False)
```

```python
import functools

import jax
import jax.numpy as jnp
from jax import lax
from jax.experimental import pallas as pl
from jax.experimental.pallas import tpu as pltpu
from jax.sharding import Mesh
from jax.sharding import PartitionSpec as P

HEAD_DIM = 128
SEGMENT_MAX = 1024
LSE_TERMS = 3
COPIES = 16
TP = ("z", "xh")
SP = ("y", "xl", "core")
F32 = jnp.float32
BF16 = jnp.bfloat16
NT = (((1,), (1,)), ((), ()))
TN = (((0,), (0,)), ((), ()))


def dot(a, b, dims=(((1,), (0,)), ((), ()))):
    return lax.dot_general(a, b, dims, preferred_element_type=F32)


def fetch(sources, targets, sems):
    copies = [
        pltpu.make_async_copy(src, dst, sems.at[i])
        for i, (src, dst) in enumerate(zip(sources, targets, strict=True))
    ]
    for copy in copies:
        copy.start()
    for copy in copies:
        copy.wait()


def window_parts(core_ref, chips, whole_ref, rows):
    mine, other = [], []
    for i in chips:
        mine.append(whole_ref.at[pl.ds(pl.multiple_of((2 * i + core_ref[0]) * rows, rows), rows)])
        other.append(
            whole_ref.at[pl.ds(pl.multiple_of((2 * i + 1 - core_ref[0]) * rows, rows), rows)]
        )
    return mine + other


def split_parts(n, refs, rows):
    return [*refs[:n], *(refs[n].at[pl.ds(i * rows, rows)] for i in range(n))]


def forward_kernel(n, core_ref, qseg_ref, kseg_ref, q_hbm, *refs):
    kv_hbm, (attn_ref, probs_ref, qx_ref, q_ref, kv_ref, sems) = refs[: n + 1], refs[n + 1 :]
    rows, width = q_ref.shape
    keys = 2 * rows * n
    chips = range(n - 1, -1, -1)
    fetch(
        (q_hbm, *split_parts(n, kv_hbm, rows)),
        (q_ref, *window_parts(core_ref, chips, kv_ref, rows)),
        sems,
    )
    scale = HEAD_DIM ** (-0.5)
    first = keys - 2 * rows + core_ref[0] * rows
    place = lax.broadcasted_iota(jnp.int32, (rows, keys), 0) + first
    allowed = (place >= lax.broadcasted_iota(jnp.int32, (rows, keys), 1)) & (
        qseg_ref[...] == kseg_ref[...]
    )
    lane = lax.broadcasted_iota(jnp.int32, (rows, HEAD_DIM), 1)
    terms = jnp.zeros((rows, HEAD_DIM), F32)
    for h in range(width // HEAD_DIM):
        cols = slice(h * HEAD_DIM, (h + 1) * HEAD_DIM)
        vcols = slice(width + h * HEAD_DIM, width + (h + 1) * HEAD_DIM)
        scores = jnp.where(allowed, dot(q_ref[:, cols], kv_ref[:, cols], NT) * scale, -1e30)
        top = jnp.max(scores, axis=-1, keepdims=True)
        expo = jnp.exp(scores - top)
        total = jnp.sum(expo, axis=-1, keepdims=True)
        probs = expo / total
        probs_ref[h] = probs
        attn_ref[:, cols] = dot(probs.astype(BF16), kv_ref[:, vcols]).astype(BF16)
        rest = top + jnp.log(total)
        for t in range(LSE_TERMS):
            term = rest.astype(BF16).astype(F32)
            rest = rest - term
            terms = jnp.where(lane == h * LSE_TERMS + t, term, terms)
    qx_ref[:, :width] = q_ref[...]
    qx_ref[:, width:] = terms.astype(BF16)


def query_grad_kernel(n, core_ref, dattn_hbm, attn_hbm, probs_hbm, *refs):
    kv_hbm, (dq_ref, dattn_ref, attn_ref, probs_ref, kv_ref, sems) = refs[: n + 1], refs[n + 1 :]
    rows, width = attn_ref.shape
    fetch(
        (dattn_hbm, attn_hbm, probs_hbm, *split_parts(n, kv_hbm, rows)),
        (
            dattn_ref,
            attn_ref,
            probs_ref,
            *window_parts(core_ref, range(n - 1, -1, -1), kv_ref, rows),
        ),
        sems,
    )
    scale = HEAD_DIM ** (-0.5)
    for h in range(width // HEAD_DIM):
        cols = slice(h * HEAD_DIM, (h + 1) * HEAD_DIM)
        vcols = slice(width + h * HEAD_DIM, width + (h + 1) * HEAD_DIM)
        dattn = dattn_ref[:, cols]
        delta = jnp.sum(
            dattn.astype(F32) * attn_ref[:, cols].astype(F32), axis=-1, keepdims=True
        )
        dprobs = dot(dattn, kv_ref[:, vcols], NT)
        dscores = (probs_ref[h] * (dprobs - delta) * scale).astype(BF16)
        dq_ref[:, cols] = dot(dscores, kv_ref[:, cols]).astype(BF16)


def key_grad_kernel(n, core_ref, qseg_ref, kseg_ref, kv_hbm, qx_hbm, attn_hbm, *refs):
    dattn_hbm, refs = refs[: n + 1], refs[n + 1 :]
    dkey_ref, dvalue_ref, kv_ref, qx_ref, attn_ref, dattn_ref, sems = refs
    rows, width = dkey_ref.shape
    queries = 2 * rows * n
    fetch(
        (kv_hbm, qx_hbm, attn_hbm, *split_parts(n, dattn_hbm, rows)),
        (kv_ref, qx_ref, attn_ref, *window_parts(core_ref, range(n), dattn_ref, rows)),
        sems,
    )
    scale = HEAD_DIM ** (-0.5)
    place = lax.broadcasted_iota(jnp.int32, (queries, rows), 1) + core_ref[0] * rows
    allowed = (lax.broadcasted_iota(jnp.int32, (queries, rows), 0) >= place) & (
        qseg_ref[...] == kseg_ref[...]
    )
    for h in range(width // HEAD_DIM):
        cols = slice(h * HEAD_DIM, (h + 1) * HEAD_DIM)
        vcols = slice(width + h * HEAD_DIM, width + (h + 1) * HEAD_DIM)
        terms = qx_ref[:, width : width + HEAD_DIM].astype(F32)
        lse = terms[:, h * LSE_TERMS : h * LSE_TERMS + 1]
        for t in range(1, LSE_TERMS):
            lse = lse + terms[:, h * LSE_TERMS + t : h * LSE_TERMS + t + 1]
        query, dattn = qx_ref[:, cols], dattn_ref[:, cols]
        scores = dot(query, kv_ref[:, cols], NT) * scale
        probs = jnp.exp(jnp.where(allowed, scores - lse, -1e30))
        delta = jnp.sum(
            dattn.astype(F32) * attn_ref[:, cols].astype(F32), axis=-1, keepdims=True
        )
        dprobs = dot(dattn, kv_ref[:, vcols], NT)
        dscores = (probs * (dprobs - delta) * scale).astype(BF16)
        dkey_ref[:, cols] = dot(dscores, query, TN).astype(BF16)
        dvalue_ref[:, cols] = dot(probs.astype(BF16), dattn, TN).astype(BF16)


def dattn_kernel(n, offsets, z_ref, dpred_hbm, *refs):
    proj_hbm, (out_ref, dpred_ref, *proj_refs, sems) = refs[: len(offsets)], refs[len(offsets) :]
    fetch((dpred_hbm, *proj_hbm), (dpred_ref, *proj_refs), sems)
    first = [0] * n
    for ref, by in zip(proj_refs, offsets, strict=True):
        size = ref.shape[0]
        z = lax.rem(z_ref[0] + by, n)
        out = dot(dpred_ref[...], ref[...], NT).astype(BF16)
        out_ref[z, :, first[by] : first[by] + size] = out
        first[by] += size


def call(kernel, out_shape, in_smem, in_vmem, in_hbm, scratch):
    space = pl.BlockSpec
    return pl.pallas_call(
        kernel,
        out_shape=out_shape,
        in_specs=[space(memory_space=pltpu.SMEM)] * len(in_smem)
        + [space(memory_space=pltpu.VMEM)] * len(in_vmem)
        + [space(memory_space=pltpu.HBM)] * len(in_hbm),
        scratch_shapes=[pltpu.VMEM(s.shape, s.dtype) for s in scratch]
        + [pltpu.SemaphoreType.DMA((COPIES,))],
        compiler_params=pltpu.CompilerParams(vmem_limit_bytes=40 * 1024 * 1024),
    )(*in_smem, *in_vmem, *in_hbm)


def body(context, w_out, teacher_resid, queries, keys, values, segment_ids, proj):
    rows, width = queries.shape
    heads = width // HEAD_DIM
    n_sp, n_z, n_xh = lax.axis_size(SP), lax.axis_size("z"), lax.axis_size("xh")
    n_core = lax.axis_size("core")
    n_chip = n_sp // n_core
    near = min(-(-(SEGMENT_MAX - 1) // (n_core * rows)), n_chip - 1) + 1
    window = near * n_core * rows
    sp, core = lax.axis_index(SP), lax.axis_index("core")
    first_row, chip_row = sp * rows, (sp - core) * rows
    z, xh = lax.axis_index("z"), lax.axis_index("xh")
    core_scalar = core[None]

    def shift(array, by):
        by = by * n_core
        pairs = [(i, i + by) for i in range(n_sp) if 0 <= i + by < n_sp]
        return lax.ppermute(array, SP, pairs)

    def other_core(arrays):
        stacked = jnp.concatenate(arrays, axis=0)
        return lax.ppermute(stacked, "core", [(i, i ^ 1) for i in range(n_core)])

    def everywhere(array):
        copies = jnp.broadcast_to(array[None], (n_sp, *array.shape))
        return lax.all_to_all(copies, SP, 0, 0, tiled=True).reshape(-1, array.shape[1])

    def turn(array, by):
        return lax.ppermute(array, "z", [(i, (i + by) % n_z) for i in range(n_z)])

    def swap(array):
        return lax.ppermute(array, "xh", [(i, i ^ 1) for i in range(n_xh)])

    context_all = lax.all_gather(context, SP, axis=0, tiled=True)

    half = width // 2
    pieces, offsets = [proj], [0]

    def step(up, down):
        k = len(pieces) // 2 + 1
        if k == n_z // 2:
            up, down = up[:half], down[half:]
        offsets.extend([n_z - k, k])
        return turn(up, 1), turn(down, -1)

    key_value = jnp.concatenate([keys, values], axis=1)
    shifted = [shift(key_value, k) for k in range(1, near)]
    up, down = step(proj, proj)
    key_value, up, down = lax.optimization_barrier((key_value, up, down))
    pieces += [up, down]
    kv_parts = (key_value, *shifted, other_core([key_value, *shifted]))

    nobody = jnp.full((window - n_core * rows,), -1, jnp.int32)
    key_segments = lax.dynamic_slice_in_dim(
        jnp.concatenate([nobody, segment_ids]), chip_row, window, 0
    )
    query_segments = lax.dynamic_slice_in_dim(
        jnp.concatenate([segment_ids, nobody]), chip_row, window, 0
    )
    own_segments = lax.dynamic_slice_in_dim(segment_ids, first_row, rows, 0)
    block_type = jax.ShapeDtypeStruct((rows, width), BF16)
    window_type = jax.ShapeDtypeStruct((window, width), BF16)
    window_kv_type = jax.ShapeDtypeStruct((window, 2 * width), BF16)
    window_qx_type = jax.ShapeDtypeStruct((window, width + HEAD_DIM), BF16)
    probs_type = jax.ShapeDtypeStruct((heads, rows, window), F32)
    attn, probs, qx = call(
        functools.partial(forward_kernel, near),
        (block_type, probs_type, jax.ShapeDtypeStruct((rows, width + HEAD_DIM), BF16)),
        (core_scalar,),
        (own_segments[:, None], key_segments[None, :]),
        (queries, *kv_parts),
        (block_type, window_kv_type),
    )
    attn_all = everywhere(attn)
    up, down = step(up, down)
    attn_all, qx, up, down = lax.optimization_barrier((attn_all, qx, up, down))
    pieces += [up, down]

    def after(array):
        array = jnp.pad(array, ((0, window - n_core * rows), (0, 0)))
        return lax.dynamic_slice_in_dim(array, chip_row, window, 0)

    qx_after, attn_after = after(everywhere(qx)), after(attn_all)

    resid_other = swap(teacher_resid)
    resid = jnp.concatenate(
        [
            jnp.where(xh == 0, teacher_resid, resid_other),
            jnp.where(xh == 0, resid_other, teacher_resid),
        ],
        axis=0,
    )
    part = (dot(attn_all, proj) - dot(context_all, w_out)).astype(BF16)
    part = lax.psum_scatter(part, "z", scatter_dimension=0, tiled=True)
    while len(pieces) < n_z:
        up, down = step(up, down)
        pieces += [up, down]
    part, resid, up, down, qx_after, attn_after = lax.optimization_barrier(
        (part, resid, up, down, qx_after, attn_after)
    )
    pieces[-2:] = [up, down]
    diff = (part.astype(F32) + swap(part).astype(F32)) - resid.astype(F32)
    dpred = diff.astype(BF16)

    dattn_part = call(
        functools.partial(dattn_kernel, n_z, offsets),
        jax.ShapeDtypeStruct((n_z, n_xh * rows, width), BF16),
        (z[None],),
        (),
        (dpred, *pieces),
        (dpred, *pieces),
    )
    dattn_parts = lax.all_to_all(dattn_part.reshape(n_sp, rows, width), SP, 0, 0, tiled=True)
    dattn = jnp.sum(dattn_parts.astype(F32), axis=0).astype(BF16)
    pairs = []
    for a in range(n_z):
        for x in range(n_xh):
            for b in range(n_z):
                for e in range(n_xh):
                    pairs.append(
                        (
                            (a * n_xh + x) * n_sp + b * n_xh + e,
                            (b * n_xh + x) * n_sp + a * n_xh + e,
                        )
                    )
    dattn = lax.ppermute(dattn, TP + SP, pairs)

    dpred_all = lax.all_gather(dpred, "z", axis=0, tiled=True)
    proj_grad = dot(attn_all, dpred_all, TN).astype(BF16)

    shifted = [shift(dattn, -k) for k in range(1, near)]
    query_grad = call(
        functools.partial(query_grad_kernel, near),
        block_type,
        (core_scalar,),
        (),
        (dattn, attn, probs, *kv_parts),
        (block_type, block_type, probs_type, window_kv_type),
    )
    key_grad, value_grad = call(
        functools.partial(key_grad_kernel, near),
        (block_type, block_type),
        (core_scalar,),
        (query_segments[:, None], own_segments[None, :]),
        (key_value, qx_after, attn_after, dattn, *shifted, other_core([dattn, *shifted])),
        (
            jax.ShapeDtypeStruct((rows, 2 * width), BF16),
            window_qx_type,
            window_type,
            window_type,
        ),
    )
    return proj_grad, query_grad, key_grad, value_grad


def solution(mesh):
    fine = Mesh(mesh.devices.reshape(8, 2, 4, 2, 2), TP + SP)
    in_specs = (
        P(SP, TP),
        P(TP, SP),
        P(TP, SP),
        P(SP, TP),
        P(SP, TP),
        P(SP, TP),
        P(),
        P(TP, SP),
    )
    out_specs = (P(TP, SP), P(SP, TP), P(SP, TP), P(SP, TP))
    return jax.shard_map(body, mesh=fine, in_specs=in_specs, out_specs=out_specs, check_vma=False)
```

```python
import functools

import jax
import jax.numpy as jnp
from jax import lax
from jax.experimental import pallas as pl
from jax.experimental.pallas import tpu as pltpu
from jax.sharding import Mesh
from jax.sharding import PartitionSpec as P

HEAD_DIM = 128
SEGMENT_MAX = 1024
LSE_TERMS = 3
COPIES = 16
TP = ("z", "xh")
SP = ("y", "xl", "core")
F32 = jnp.float32
BF16 = jnp.bfloat16
NT = (((1,), (1,)), ((), ()))
TN = (((0,), (0,)), ((), ()))


def dot(a, b, dims=(((1,), (0,)), ((), ()))):
    return lax.dot_general(a, b, dims, preferred_element_type=F32)


def fetch(sources, targets, sems):
    copies = [
        pltpu.make_async_copy(src, dst, sems.at[i])
        for i, (src, dst) in enumerate(zip(sources, targets, strict=True))
    ]
    for copy in copies:
        copy.start()
    for copy in copies:
        copy.wait()


def window_parts(core_ref, chips, whole_ref, rows):
    mine, other = [], []
    for i in chips:
        mine.append(whole_ref.at[pl.ds(pl.multiple_of((2 * i + core_ref[0]) * rows, rows), rows)])
        other.append(
            whole_ref.at[pl.ds(pl.multiple_of((2 * i + 1 - core_ref[0]) * rows, rows), rows)]
        )
    return mine + other


def split_parts(n, refs, rows):
    return [*refs[:n], *(refs[n].at[pl.ds(i * rows, rows)] for i in range(n))]


def forward_kernel(n, core_ref, qseg_ref, kseg_ref, q_hbm, *refs):
    kv_hbm, (attn_ref, probs_ref, qx_ref, q_ref, kv_ref, sems) = refs[: n + 1], refs[n + 1 :]
    rows, width = q_ref.shape
    keys = 2 * rows * n
    chips = range(n - 1, -1, -1)
    fetch(
        (q_hbm, *split_parts(n, kv_hbm, rows)),
        (q_ref, *window_parts(core_ref, chips, kv_ref, rows)),
        sems,
    )
    scale = HEAD_DIM ** (-0.5)
    first = keys - 2 * rows + core_ref[0] * rows
    place = lax.broadcasted_iota(jnp.int32, (rows, keys), 0) + first
    allowed = (place >= lax.broadcasted_iota(jnp.int32, (rows, keys), 1)) & (
        qseg_ref[...] == kseg_ref[...]
    )
    lane = lax.broadcasted_iota(jnp.int32, (rows, HEAD_DIM), 1)
    terms = jnp.zeros((rows, HEAD_DIM), F32)
    for h in range(width // HEAD_DIM):
        cols = slice(h * HEAD_DIM, (h + 1) * HEAD_DIM)
        vcols = slice(width + h * HEAD_DIM, width + (h + 1) * HEAD_DIM)
        scores = jnp.where(allowed, dot(q_ref[:, cols], kv_ref[:, cols], NT) * scale, -1e30)
        top = jnp.max(scores, axis=-1, keepdims=True)
        expo = jnp.exp(scores - top)
        total = jnp.sum(expo, axis=-1, keepdims=True)
        probs = expo / total
        probs_ref[h] = probs
        attn_ref[:, cols] = dot(probs.astype(BF16), kv_ref[:, vcols]).astype(BF16)
        rest = top + jnp.log(total)
        for t in range(LSE_TERMS):
            term = rest.astype(BF16).astype(F32)
            rest = rest - term
            terms = jnp.where(lane == h * LSE_TERMS + t, term, terms)
    qx_ref[:, :width] = q_ref[...]
    qx_ref[:, width:] = terms.astype(BF16)


def query_grad_kernel(n, core_ref, dattn_hbm, attn_hbm, probs_hbm, *refs):
    kv_hbm, (dq_ref, dattn_ref, attn_ref, probs_ref, kv_ref, sems) = refs[: n + 1], refs[n + 1 :]
    rows, width = attn_ref.shape
    fetch(
        (dattn_hbm, attn_hbm, probs_hbm, *split_parts(n, kv_hbm, rows)),
        (
            dattn_ref,
            attn_ref,
            probs_ref,
            *window_parts(core_ref, range(n - 1, -1, -1), kv_ref, rows),
        ),
        sems,
    )
    scale = HEAD_DIM ** (-0.5)
    for h in range(width // HEAD_DIM):
        cols = slice(h * HEAD_DIM, (h + 1) * HEAD_DIM)
        vcols = slice(width + h * HEAD_DIM, width + (h + 1) * HEAD_DIM)
        dattn = dattn_ref[:, cols]
        delta = jnp.sum(
            dattn.astype(F32) * attn_ref[:, cols].astype(F32), axis=-1, keepdims=True
        )
        dprobs = dot(dattn, kv_ref[:, vcols], NT)
        dscores = (probs_ref[h] * (dprobs - delta) * scale).astype(BF16)
        dq_ref[:, cols] = dot(dscores, kv_ref[:, cols]).astype(BF16)


def key_grad_kernel(n, core_ref, qseg_ref, kseg_ref, kv_hbm, qx_hbm, attn_hbm, *refs):
    dattn_hbm, refs = refs[: n + 1], refs[n + 1 :]
    dkey_ref, dvalue_ref, kv_ref, qx_ref, attn_ref, dattn_ref, sems = refs
    rows, width = dkey_ref.shape
    queries = 2 * rows * n
    fetch(
        (kv_hbm, qx_hbm, attn_hbm, *split_parts(n, dattn_hbm, rows)),
        (kv_ref, qx_ref, attn_ref, *window_parts(core_ref, range(n), dattn_ref, rows)),
        sems,
    )
    scale = HEAD_DIM ** (-0.5)
    place = lax.broadcasted_iota(jnp.int32, (queries, rows), 1) + core_ref[0] * rows
    allowed = (lax.broadcasted_iota(jnp.int32, (queries, rows), 0) >= place) & (
        qseg_ref[...] == kseg_ref[...]
    )
    for h in range(width // HEAD_DIM):
        cols = slice(h * HEAD_DIM, (h + 1) * HEAD_DIM)
        vcols = slice(width + h * HEAD_DIM, width + (h + 1) * HEAD_DIM)
        terms = qx_ref[:, width : width + HEAD_DIM].astype(F32)
        lse = terms[:, h * LSE_TERMS : h * LSE_TERMS + 1]
        for t in range(1, LSE_TERMS):
            lse = lse + terms[:, h * LSE_TERMS + t : h * LSE_TERMS + t + 1]
        query, dattn = qx_ref[:, cols], dattn_ref[:, cols]
        scores = dot(query, kv_ref[:, cols], NT) * scale
        probs = jnp.exp(jnp.where(allowed, scores - lse, -1e30))
        delta = jnp.sum(
            dattn.astype(F32) * attn_ref[:, cols].astype(F32), axis=-1, keepdims=True
        )
        dprobs = dot(dattn, kv_ref[:, vcols], NT)
        dscores = (probs * (dprobs - delta) * scale).astype(BF16)
        dkey_ref[:, cols] = dot(dscores, query, TN).astype(BF16)
        dvalue_ref[:, cols] = dot(probs.astype(BF16), dattn, TN).astype(BF16)


def dattn_kernel(n, offsets, z_ref, dpred_hbm, *refs):
    proj_hbm, (out_ref, dpred_ref, *proj_refs, sems) = refs[: len(offsets)], refs[len(offsets) :]
    fetch((dpred_hbm, *proj_hbm), (dpred_ref, *proj_refs), sems)
    first = [0] * n
    for ref, by in zip(proj_refs, offsets, strict=True):
        size = ref.shape[0]
        z = lax.rem(z_ref[0] + by, n)
        out = dot(dpred_ref[...], ref[...], NT).astype(BF16)
        out_ref[z, :, first[by] : first[by] + size] = out
        first[by] += size


def difference_kernel(attn_ref, proj_ref, teacher_ref, out_ref):
    out = dot(attn_ref[...], proj_ref[...]) - teacher_ref[...].astype(F32)
    out_ref[...] = out.astype(BF16)


def difference(attn, proj, teacher):
    tokens, depth = attn.shape
    features = proj.shape[1]
    step = tokens // 8
    return pl.pallas_call(
        difference_kernel,
        out_shape=pltpu.HBM((tokens, features), BF16),
        grid=(tokens // step,),
        in_specs=[
            pl.BlockSpec((step, depth), lambda i: (i, 0)),
            pl.BlockSpec((depth, features), lambda i: (0, 0)),
            pl.BlockSpec((step, features), lambda i: (i, 0)),
        ],
        out_specs=pl.BlockSpec((step, features), lambda i: (i, 0)),
        compiler_params=pltpu.CompilerParams(vmem_limit_bytes=16 * 1024 * 1024),
    )(*(pltpu.with_memory_space_constraint(x, pltpu.HBM) for x in (attn, proj, teacher)))


def call(kernel, out_shape, in_smem, in_vmem, in_hbm, scratch):
    space = pl.BlockSpec
    in_hbm = [pltpu.with_memory_space_constraint(x, pltpu.HBM) for x in in_hbm]
    return pl.pallas_call(
        kernel,
        out_shape=out_shape,
        in_specs=[space(memory_space=pltpu.SMEM)] * len(in_smem)
        + [space(memory_space=pltpu.VMEM)] * len(in_vmem)
        + [space(memory_space=pltpu.HBM)] * len(in_hbm),
        scratch_shapes=[pltpu.VMEM(s.shape, s.dtype) for s in scratch]
        + [pltpu.SemaphoreType.DMA((COPIES,))],
        compiler_params=pltpu.CompilerParams(vmem_limit_bytes=16 * 1024 * 1024),
    )(*in_smem, *in_vmem, *in_hbm)


def body(context, w_out, teacher_resid, queries, keys, values, segment_ids, proj):
    rows, width = queries.shape
    heads = width // HEAD_DIM
    n_sp, n_z, n_xh = lax.axis_size(SP), lax.axis_size("z"), lax.axis_size("xh")
    n_core = lax.axis_size("core")
    n_chip = n_sp // n_core
    near = min(-(-(SEGMENT_MAX - 1) // (n_core * rows)), n_chip - 1) + 1
    window = near * n_core * rows
    sp, core = lax.axis_index(SP), lax.axis_index("core")
    first_row, chip_row = sp * rows, (sp - core) * rows
    z, xh = lax.axis_index("z"), lax.axis_index("xh")
    core_scalar = core[None]

    def shift(array, by):
        by = by * n_core
        pairs = [(i, i + by) for i in range(n_sp) if 0 <= i + by < n_sp]
        return lax.ppermute(array, SP, pairs)

    def other_core(arrays):
        stacked = jnp.concatenate(arrays, axis=0)
        return lax.ppermute(stacked, "core", [(i, i ^ 1) for i in range(n_core)])

    def everywhere(array):
        copies = jnp.broadcast_to(array[None], (n_sp, *array.shape))
        return lax.all_to_all(copies, SP, 0, 0, tiled=True).reshape(-1, array.shape[1])

    def turn(array, by):
        return lax.ppermute(array, "z", [(i, (i + by) % n_z) for i in range(n_z)])

    def swap(array):
        return lax.ppermute(array, "xh", [(i, i ^ 1) for i in range(n_xh)])

    context_all = lax.all_gather(context, SP, axis=0, tiled=True)

    half = width // 2
    pieces, offsets = [proj], [0]

    def step(up, down):
        k = len(pieces) // 2 + 1
        offsets.extend([n_z - k, k])
        return turn(up, 1), turn(down, -1)

    key_value = jnp.concatenate([keys, values], axis=1)
    shifted = [shift(key_value, k) for k in range(1, near)]
    up, down = step(proj, proj)
    key_value, up, down = lax.optimization_barrier((key_value, up, down))
    pieces += [up, down]
    kv_parts = (key_value, *shifted, other_core([key_value, *shifted]))

    nobody = jnp.full((window - n_core * rows,), -1, jnp.int32)
    key_segments = lax.dynamic_slice_in_dim(
        jnp.concatenate([nobody, segment_ids]), chip_row, window, 0
    )
    query_segments = lax.dynamic_slice_in_dim(
        jnp.concatenate([segment_ids, nobody]), chip_row, window, 0
    )
    own_segments = lax.dynamic_slice_in_dim(segment_ids, first_row, rows, 0)
    block_type = jax.ShapeDtypeStruct((rows, width), BF16)
    window_type = jax.ShapeDtypeStruct((window, width), BF16)
    window_kv_type = jax.ShapeDtypeStruct((window, 2 * width), BF16)
    window_qx_type = jax.ShapeDtypeStruct((window, width + HEAD_DIM), BF16)
    probs_type = jax.ShapeDtypeStruct((heads, rows, window), F32)
    attn, probs, qx = call(
        functools.partial(forward_kernel, near),
        (block_type, probs_type, jax.ShapeDtypeStruct((rows, width + HEAD_DIM), BF16)),
        (core_scalar,),
        (own_segments[:, None], key_segments[None, :]),
        (queries, *kv_parts),
        (block_type, window_kv_type),
    )
    attn_all = everywhere(attn)
    up, down = step(up, down)
    pieces += [up, down]
    up, down = step(up, down)
    teacher_part = dot(context_all, w_out).astype(BF16)
    teacher_part, qx, up, down = lax.optimization_barrier((teacher_part, qx, up, down))
    pieces += [up, down]

    def after(array):
        array = jnp.pad(array, ((0, window - n_core * rows), (0, 0)))
        return lax.dynamic_slice_in_dim(array, chip_row, window, 0)

    qx_after, attn_after = after(everywhere(qx)), after(attn_all)

    resid_other = swap(teacher_resid)
    resid = jnp.concatenate(
        [
            jnp.where(xh == 0, teacher_resid, resid_other),
            jnp.where(xh == 0, resid_other, teacher_resid),
        ],
        axis=0,
    )
    part = difference(attn_all, proj, teacher_part)
    part = lax.psum_scatter(part, "z", scatter_dimension=0, tiled=True)
    up, down = up[:half], down[half:]
    part, resid, qx_after, attn_after, up, down = lax.optimization_barrier(
        (part, resid, qx_after, attn_after, up, down)
    )
    part_other = swap(part)
    up, down = step(up, down)
    part_other, up, down = lax.optimization_barrier((part_other, up, down))
    pieces += [up, down]
    diff = (part.astype(F32) + part_other.astype(F32)) - resid.astype(F32)
    dpred = diff.astype(BF16)

    dattn_part = call(
        functools.partial(dattn_kernel, n_z, offsets),
        jax.ShapeDtypeStruct((n_z, n_xh * rows, width), BF16),
        (z[None],),
        (),
        (dpred, *pieces),
        (dpred, *pieces),
    )
    dattn_parts = lax.all_to_all(dattn_part.reshape(n_sp, rows, width), SP, 0, 0, tiled=True)
    dattn = jnp.sum(dattn_parts.astype(F32), axis=0).astype(BF16)
    pairs = []
    for a in range(n_z):
        for x in range(n_xh):
            for b in range(n_z):
                for e in range(n_xh):
                    pairs.append(
                        (
                            (a * n_xh + x) * n_sp + b * n_xh + e,
                            (b * n_xh + x) * n_sp + a * n_xh + e,
                        )
                    )
    dattn = lax.ppermute(dattn, TP + SP, pairs)

    dpred_all = lax.all_gather(dpred, "z", axis=0, tiled=True)
    proj_grad = dot(attn_all, dpred_all, TN).astype(BF16)

    shifted = [shift(dattn, -k) for k in range(1, near)]
    query_grad = call(
        functools.partial(query_grad_kernel, near),
        block_type,
        (core_scalar,),
        (),
        (dattn, attn, probs, *kv_parts),
        (block_type, block_type, probs_type, window_kv_type),
    )
    key_value, query_grad = lax.optimization_barrier((key_value, query_grad))
    key_grad, value_grad = call(
        functools.partial(key_grad_kernel, near),
        (block_type, block_type),
        (core_scalar,),
        (query_segments[:, None], own_segments[None, :]),
        (key_value, qx_after, attn_after, dattn, *shifted, other_core([dattn, *shifted])),
        (
            jax.ShapeDtypeStruct((rows, 2 * width), BF16),
            window_qx_type,
            window_type,
            window_type,
        ),
    )
    return proj_grad, query_grad, key_grad, value_grad


def solution(mesh):
    fine = Mesh(mesh.devices.reshape(8, 2, 4, 2, 2), TP + SP)
    in_specs = (
        P(SP, TP),
        P(TP, SP),
        P(TP, SP),
        P(SP, TP),
        P(SP, TP),
        P(SP, TP),
        P(),
        P(TP, SP),
    )
    out_specs = (P(TP, SP), P(SP, TP), P(SP, TP), P(SP, TP))
    return jax.shard_map(body, mesh=fine, in_specs=in_specs, out_specs=out_specs, check_vma=False)
```

```python
import functools

import jax
import jax.numpy as jnp
from jax import lax
from jax.experimental import pallas as pl
from jax.experimental.pallas import tpu as pltpu
from jax.sharding import Mesh
from jax.sharding import PartitionSpec as P

HEAD_DIM = 128
SEGMENT_MAX = 1024
LSE_TERMS = 3
COPIES = 16
TP = ("z", "xh")
SP = ("y", "xl", "core")
F32 = jnp.float32
BF16 = jnp.bfloat16
NT = (((1,), (1,)), ((), ()))
TN = (((0,), (0,)), ((), ()))


def dot(a, b, dims=(((1,), (0,)), ((), ()))):
    return lax.dot_general(a, b, dims, preferred_element_type=F32)


def fetch(sources, targets, sems):
    copies = [
        pltpu.make_async_copy(src, dst, sems.at[i])
        for i, (src, dst) in enumerate(zip(sources, targets, strict=True))
    ]
    for copy in copies:
        copy.start()
    for copy in copies:
        copy.wait()


def window_parts(core_ref, chips, whole_ref, rows):
    mine, other = [], []
    for i in chips:
        mine.append(whole_ref.at[pl.ds(pl.multiple_of((2 * i + core_ref[0]) * rows, rows), rows)])
        other.append(
            whole_ref.at[pl.ds(pl.multiple_of((2 * i + 1 - core_ref[0]) * rows, rows), rows)]
        )
    return mine + other


def split_parts(n, refs, rows):
    return [*refs[:n], *(refs[n].at[pl.ds(i * rows, rows)] for i in range(n))]


def forward_kernel(n, core_ref, qseg_ref, kseg_ref, q_hbm, *refs):
    kv_hbm, (attn_ref, probs_ref, qx_ref, q_ref, kv_ref, sems) = refs[: n + 1], refs[n + 1 :]
    rows, width = q_ref.shape
    keys = 2 * rows * n
    chips = range(n - 1, -1, -1)
    fetch(
        (q_hbm, *split_parts(n, kv_hbm, rows)),
        (q_ref, *window_parts(core_ref, chips, kv_ref, rows)),
        sems,
    )
    scale = HEAD_DIM ** (-0.5)
    first = keys - 2 * rows + core_ref[0] * rows
    place = lax.broadcasted_iota(jnp.int32, (rows, keys), 0) + first
    allowed = (place >= lax.broadcasted_iota(jnp.int32, (rows, keys), 1)) & (
        qseg_ref[...] == kseg_ref[...]
    )
    lane = lax.broadcasted_iota(jnp.int32, (rows, HEAD_DIM), 1)
    terms = jnp.zeros((rows, HEAD_DIM), F32)
    for h in range(width // HEAD_DIM):
        cols = slice(h * HEAD_DIM, (h + 1) * HEAD_DIM)
        vcols = slice(width + h * HEAD_DIM, width + (h + 1) * HEAD_DIM)
        scores = jnp.where(allowed, dot(q_ref[:, cols], kv_ref[:, cols], NT) * scale, -1e30)
        top = jnp.max(scores, axis=-1, keepdims=True)
        expo = jnp.exp(scores - top)
        total = jnp.sum(expo, axis=-1, keepdims=True)
        probs = expo / total
        probs_ref[h] = probs
        attn_ref[:, cols] = dot(probs.astype(BF16), kv_ref[:, vcols]).astype(BF16)
        rest = top + jnp.log(total)
        for t in range(LSE_TERMS):
            term = rest.astype(BF16).astype(F32)
            rest = rest - term
            terms = jnp.where(lane == h * LSE_TERMS + t, term, terms)
    qx_ref[:, :width] = q_ref[...]
    qx_ref[:, width:] = terms.astype(BF16)


def query_grad_kernel(n, core_ref, dattn_hbm, attn_hbm, probs_hbm, *refs):
    kv_hbm, (dq_ref, dattn_ref, attn_ref, probs_ref, kv_ref, sems) = refs[: n + 1], refs[n + 1 :]
    rows, width = attn_ref.shape
    fetch(
        (dattn_hbm, attn_hbm, probs_hbm, *split_parts(n, kv_hbm, rows)),
        (
            dattn_ref,
            attn_ref,
            probs_ref,
            *window_parts(core_ref, range(n - 1, -1, -1), kv_ref, rows),
        ),
        sems,
    )
    scale = HEAD_DIM ** (-0.5)
    for h in range(width // HEAD_DIM):
        cols = slice(h * HEAD_DIM, (h + 1) * HEAD_DIM)
        vcols = slice(width + h * HEAD_DIM, width + (h + 1) * HEAD_DIM)
        dattn = dattn_ref[:, cols]
        delta = jnp.sum(
            dattn.astype(F32) * attn_ref[:, cols].astype(F32), axis=-1, keepdims=True
        )
        dprobs = dot(dattn, kv_ref[:, vcols], NT)
        dscores = (probs_ref[h] * (dprobs - delta) * scale).astype(BF16)
        dq_ref[:, cols] = dot(dscores, kv_ref[:, cols]).astype(BF16)


def key_grad_kernel(n, core_ref, qseg_ref, kseg_ref, kv_hbm, qx_hbm, attn_hbm, *refs):
    dattn_hbm, refs = refs[: n + 1], refs[n + 1 :]
    dkey_ref, dvalue_ref, kv_ref, qx_ref, attn_ref, dattn_ref, sems = refs
    rows, width = dkey_ref.shape
    queries = 2 * rows * n
    fetch(
        (kv_hbm, qx_hbm, attn_hbm, *split_parts(n, dattn_hbm, rows)),
        (kv_ref, qx_ref, attn_ref, *window_parts(core_ref, range(n), dattn_ref, rows)),
        sems,
    )
    scale = HEAD_DIM ** (-0.5)
    place = lax.broadcasted_iota(jnp.int32, (queries, rows), 1) + core_ref[0] * rows
    allowed = (lax.broadcasted_iota(jnp.int32, (queries, rows), 0) >= place) & (
        qseg_ref[...] == kseg_ref[...]
    )
    for h in range(width // HEAD_DIM):
        cols = slice(h * HEAD_DIM, (h + 1) * HEAD_DIM)
        vcols = slice(width + h * HEAD_DIM, width + (h + 1) * HEAD_DIM)
        terms = qx_ref[:, width : width + HEAD_DIM].astype(F32)
        lse = terms[:, h * LSE_TERMS : h * LSE_TERMS + 1]
        for t in range(1, LSE_TERMS):
            lse = lse + terms[:, h * LSE_TERMS + t : h * LSE_TERMS + t + 1]
        query, dattn = qx_ref[:, cols], dattn_ref[:, cols]
        scores = dot(query, kv_ref[:, cols], NT) * scale
        probs = jnp.exp(jnp.where(allowed, scores - lse, -1e30))
        delta = jnp.sum(
            dattn.astype(F32) * attn_ref[:, cols].astype(F32), axis=-1, keepdims=True
        )
        dprobs = dot(dattn, kv_ref[:, vcols], NT)
        dscores = (probs * (dprobs - delta) * scale).astype(BF16)
        dkey_ref[:, cols] = dot(dscores, query, TN).astype(BF16)
        dvalue_ref[:, cols] = dot(probs.astype(BF16), dattn, TN).astype(BF16)


def dattn_kernel(n, offsets, z_ref, dpred_hbm, *refs):
    proj_hbm, (out_ref, dpred_ref, *proj_refs, sems) = refs[: len(offsets)], refs[len(offsets) :]
    fetch((dpred_hbm, *proj_hbm), (dpred_ref, *proj_refs), sems)
    first = [0] * n
    for ref, by in zip(proj_refs, offsets, strict=True):
        size = ref.shape[0]
        z = lax.rem(z_ref[0] + by, n)
        out = dot(dpred_ref[...], ref[...], NT).astype(BF16)
        out_ref[z, :, first[by] : first[by] + size] = out
        first[by] += size


def difference_kernel(n, attn_hbm, proj_hbm, teacher_hbm, out_hbm, *refs):
    attn_ref, proj_ref, teacher_ref, out_ref, sems = refs
    rows = attn_ref.shape[0] // n
    parts = [pl.ds(i * rows, rows) for i in range(n)]
    first = [
        pltpu.make_async_copy(attn_hbm, attn_ref, sems.at[2 * n]),
        pltpu.make_async_copy(proj_hbm, proj_ref, sems.at[2 * n + 1]),
    ]
    reads = [
        pltpu.make_async_copy(teacher_hbm.at[p], teacher_ref.at[p], sems.at[i])
        for i, p in enumerate(parts)
    ]
    writes = [
        pltpu.make_async_copy(out_ref.at[p], out_hbm.at[p], sems.at[n + i])
        for i, p in enumerate(parts)
    ]
    for copy in first + reads:
        copy.start()
    for copy in first:
        copy.wait()
    for i, p in enumerate(parts):
        reads[i].wait()
        out = dot(attn_ref[p, :], proj_ref[...]) - teacher_ref[p, :].astype(F32)
        out_ref[p, :] = out.astype(BF16)
        writes[i].start()
    for copy in writes:
        copy.wait()


def difference(attn, proj, teacher):
    n = 8
    hbm = pl.BlockSpec(memory_space=pltpu.HBM)
    return pl.pallas_call(
        functools.partial(difference_kernel, n),
        out_shape=pltpu.HBM(teacher.shape, BF16),
        in_specs=[hbm, hbm, hbm],
        out_specs=hbm,
        scratch_shapes=[
            pltpu.VMEM(attn.shape, BF16),
            pltpu.VMEM(proj.shape, BF16),
            pltpu.VMEM(teacher.shape, BF16),
            pltpu.VMEM(teacher.shape, BF16),
            pltpu.SemaphoreType.DMA((2 * n + 2,)),
        ],
        compiler_params=pltpu.CompilerParams(vmem_limit_bytes=24 * 1024 * 1024),
    )(*(pltpu.with_memory_space_constraint(x, pltpu.HBM) for x in (attn, proj, teacher)))


def call(kernel, out_shape, in_smem, in_vmem, in_hbm, scratch):
    space = pl.BlockSpec
    in_hbm = [pltpu.with_memory_space_constraint(x, pltpu.HBM) for x in in_hbm]
    return pl.pallas_call(
        kernel,
        out_shape=out_shape,
        in_specs=[space(memory_space=pltpu.SMEM)] * len(in_smem)
        + [space(memory_space=pltpu.VMEM)] * len(in_vmem)
        + [space(memory_space=pltpu.HBM)] * len(in_hbm),
        scratch_shapes=[pltpu.VMEM(s.shape, s.dtype) for s in scratch]
        + [pltpu.SemaphoreType.DMA((COPIES,))],
        compiler_params=pltpu.CompilerParams(vmem_limit_bytes=16 * 1024 * 1024),
    )(*in_smem, *in_vmem, *in_hbm)


def body(context, w_out, teacher_resid, queries, keys, values, segment_ids, proj):
    rows, width = queries.shape
    heads = width // HEAD_DIM
    n_sp, n_z, n_xh = lax.axis_size(SP), lax.axis_size("z"), lax.axis_size("xh")
    n_core = lax.axis_size("core")
    n_chip = n_sp // n_core
    near = min(-(-(SEGMENT_MAX - 1) // (n_core * rows)), n_chip - 1) + 1
    window = near * n_core * rows
    sp, core = lax.axis_index(SP), lax.axis_index("core")
    first_row, chip_row = sp * rows, (sp - core) * rows
    z, xh = lax.axis_index("z"), lax.axis_index("xh")
    core_scalar = core[None]

    def shift(array, by):
        by = by * n_core
        pairs = [(i, i + by) for i in range(n_sp) if 0 <= i + by < n_sp]
        return lax.ppermute(array, SP, pairs)

    def other_core(arrays):
        stacked = jnp.concatenate(arrays, axis=0)
        return lax.ppermute(stacked, "core", [(i, i ^ 1) for i in range(n_core)])

    def everywhere(array):
        copies = jnp.broadcast_to(array[None], (n_sp, *array.shape))
        return lax.all_to_all(copies, SP, 0, 0, tiled=True).reshape(-1, array.shape[1])

    def turn(array, by):
        return lax.ppermute(array, "z", [(i, (i + by) % n_z) for i in range(n_z)])

    def swap(array):
        return lax.ppermute(array, "xh", [(i, i ^ 1) for i in range(n_xh)])

    context_all = lax.all_gather(context, SP, axis=0, tiled=True)

    half = width // 2
    pieces, offsets = [proj], [0]

    def step(up, down):
        k = len(pieces) // 2 + 1
        offsets.extend([n_z - k, k])
        return turn(up, 1), turn(down, -1)

    key_value = jnp.concatenate([keys, values], axis=1)
    shifted = [shift(key_value, k) for k in range(1, near)]
    up, down = step(proj, proj)
    key_value, up, down = lax.optimization_barrier((key_value, up, down))
    pieces += [up, down]
    kv_parts = (key_value, *shifted, other_core([key_value, *shifted]))

    nobody = jnp.full((window - n_core * rows,), -1, jnp.int32)
    key_segments = lax.dynamic_slice_in_dim(
        jnp.concatenate([nobody, segment_ids]), chip_row, window, 0
    )
    query_segments = lax.dynamic_slice_in_dim(
        jnp.concatenate([segment_ids, nobody]), chip_row, window, 0
    )
    own_segments = lax.dynamic_slice_in_dim(segment_ids, first_row, rows, 0)
    block_type = jax.ShapeDtypeStruct((rows, width), BF16)
    window_type = jax.ShapeDtypeStruct((window, width), BF16)
    window_kv_type = jax.ShapeDtypeStruct((window, 2 * width), BF16)
    window_qx_type = jax.ShapeDtypeStruct((window, width + HEAD_DIM), BF16)
    probs_type = jax.ShapeDtypeStruct((heads, rows, window), F32)
    attn, probs, qx = call(
        functools.partial(forward_kernel, near),
        (block_type, probs_type, jax.ShapeDtypeStruct((rows, width + HEAD_DIM), BF16)),
        (core_scalar,),
        (own_segments[:, None], key_segments[None, :]),
        (queries, *kv_parts),
        (block_type, window_kv_type),
    )
    attn_all = everywhere(attn)
    up, down = step(up, down)
    pieces += [up, down]
    up, down = step(up, down)
    teacher_part = dot(context_all, w_out).astype(BF16)
    teacher_part, qx, up, down = lax.optimization_barrier((teacher_part, qx, up, down))
    pieces += [up, down]

    def after(array):
        array = jnp.pad(array, ((0, window - n_core * rows), (0, 0)))
        return lax.dynamic_slice_in_dim(array, chip_row, window, 0)

    qx_after, attn_after = after(everywhere(qx)), after(attn_all)

    resid_other = swap(teacher_resid)
    resid = jnp.concatenate(
        [
            jnp.where(xh == 0, teacher_resid, resid_other),
            jnp.where(xh == 0, resid_other, teacher_resid),
        ],
        axis=0,
    )
    part = difference(attn_all, proj, teacher_part)
    part = lax.psum_scatter(part, "z", scatter_dimension=0, tiled=True)
    up, down = up[:half], down[half:]
    part, resid, qx_after, attn_after, up, down = lax.optimization_barrier(
        (part, resid, qx_after, attn_after, up, down)
    )
    part_other = swap(part)
    up, down = step(up, down)
    part_other, up, down = lax.optimization_barrier((part_other, up, down))
    pieces += [up, down]
    diff = (part.astype(F32) + part_other.astype(F32)) - resid.astype(F32)
    dpred = diff.astype(BF16)

    dattn_part = call(
        functools.partial(dattn_kernel, n_z, offsets),
        jax.ShapeDtypeStruct((n_z, n_xh * rows, width), BF16),
        (z[None],),
        (),
        (dpred, *pieces),
        (dpred, *pieces),
    )
    dattn_parts = lax.all_to_all(dattn_part.reshape(n_sp, rows, width), SP, 0, 0, tiled=True)
    dattn = jnp.sum(dattn_parts.astype(F32), axis=0).astype(BF16)
    pairs = []
    for a in range(n_z):
        for x in range(n_xh):
            for b in range(n_z):
                for e in range(n_xh):
                    pairs.append(
                        (
                            (a * n_xh + x) * n_sp + b * n_xh + e,
                            (b * n_xh + x) * n_sp + a * n_xh + e,
                        )
                    )
    dattn = lax.ppermute(dattn, TP + SP, pairs)

    dpred_all = lax.all_gather(dpred, "z", axis=0, tiled=True)
    proj_grad = dot(attn_all, dpred_all, TN).astype(BF16)

    shifted = [shift(dattn, -k) for k in range(1, near)]
    query_grad = call(
        functools.partial(query_grad_kernel, near),
        block_type,
        (core_scalar,),
        (),
        (dattn, attn, probs, *kv_parts),
        (block_type, block_type, probs_type, window_kv_type),
    )
    key_value, query_grad = lax.optimization_barrier((key_value, query_grad))
    key_grad, value_grad = call(
        functools.partial(key_grad_kernel, near),
        (block_type, block_type),
        (core_scalar,),
        (query_segments[:, None], own_segments[None, :]),
        (key_value, qx_after, attn_after, dattn, *shifted, other_core([dattn, *shifted])),
        (
            jax.ShapeDtypeStruct((rows, 2 * width), BF16),
            window_qx_type,
            window_type,
            window_type,
        ),
    )
    return proj_grad, query_grad, key_grad, value_grad


def solution(mesh):
    fine = Mesh(mesh.devices.reshape(8, 2, 4, 2, 2), TP + SP)
    in_specs = (
        P(SP, TP),
        P(TP, SP),
        P(TP, SP),
        P(SP, TP),
        P(SP, TP),
        P(SP, TP),
        P(),
        P(TP, SP),
    )
    out_specs = (P(TP, SP), P(SP, TP), P(SP, TP), P(SP, TP))
    return jax.shard_map(body, mesh=fine, in_specs=in_specs, out_specs=out_specs, check_vma=False)
```

```python
import functools

import jax
import jax.numpy as jnp
from jax import lax
from jax.experimental import pallas as pl
from jax.experimental.pallas import tpu as pltpu
from jax.sharding import Mesh
from jax.sharding import PartitionSpec as P

HEAD_DIM = 128
SEGMENT_MAX = 1024
LSE_TERMS = 3
COPIES = 24
TP = ("z", "xh")
SP = ("y", "xl", "core")
F32 = jnp.float32
BF16 = jnp.bfloat16
NT = (((1,), (1,)), ((), ()))
TN = (((0,), (0,)), ((), ()))


def dot(a, b, dims=(((1,), (0,)), ((), ()))):
    return lax.dot_general(a, b, dims, preferred_element_type=F32)


def begin(sources, targets, sems, first=0):
    copies = [
        pltpu.make_async_copy(src, dst, sems.at[first + i])
        for i, (src, dst) in enumerate(zip(sources, targets, strict=True))
    ]
    for copy in copies:
        copy.start()
    return copies


def finish(copies):
    for copy in copies:
        copy.wait()


def fetch(sources, targets, sems):
    finish(begin(sources, targets, sems))


def window_parts(core_ref, chips, whole_ref, rows):
    mine, other = [], []
    for i in chips:
        mine.append(whole_ref.at[pl.ds(pl.multiple_of((2 * i + core_ref[0]) * rows, rows), rows)])
        other.append(
            whole_ref.at[pl.ds(pl.multiple_of((2 * i + 1 - core_ref[0]) * rows, rows), rows)]
        )
    return mine + other


def split_parts(n, refs, rows):
    return [*refs[:n], *(refs[n].at[pl.ds(i * rows, rows)] for i in range(n))]


def forward_kernel(n, core_ref, qseg_ref, kseg_ref, q_hbm, *refs):
    kv_hbm, refs = refs[: n + 1], refs[n + 1 :]
    attn_ref, probs_hbm, qx_ref, q_ref, kv_ref, probs_ref, sems = refs
    out = []
    rows, width = q_ref.shape
    keys = 2 * rows * n
    chips = range(n - 1, -1, -1)
    fetch(
        (q_hbm, *split_parts(n, kv_hbm, rows)),
        (q_ref, *window_parts(core_ref, chips, kv_ref, rows)),
        sems,
    )
    scale = HEAD_DIM ** (-0.5)
    first = keys - 2 * rows + core_ref[0] * rows
    place = lax.broadcasted_iota(jnp.int32, (rows, keys), 0) + first
    allowed = (place >= lax.broadcasted_iota(jnp.int32, (rows, keys), 1)) & (
        qseg_ref[...] == kseg_ref[...]
    )
    lane = lax.broadcasted_iota(jnp.int32, (rows, HEAD_DIM), 1)
    terms = jnp.zeros((rows, HEAD_DIM), F32)
    for h in range(width // HEAD_DIM):
        cols = slice(h * HEAD_DIM, (h + 1) * HEAD_DIM)
        vcols = slice(width + h * HEAD_DIM, width + (h + 1) * HEAD_DIM)
        scores = jnp.where(allowed, dot(q_ref[:, cols], kv_ref[:, cols], NT) * scale, -1e30)
        top = jnp.max(scores, axis=-1, keepdims=True)
        expo = jnp.exp(scores - top)
        total = jnp.sum(expo, axis=-1, keepdims=True)
        probs = expo / total
        probs_ref[h] = probs
        out += begin([probs_ref.at[h]], [probs_hbm.at[h]], sems, h)
        attn_ref[:, cols] = dot(probs.astype(BF16), kv_ref[:, vcols]).astype(BF16)
        rest = top + jnp.log(total)
        for t in range(LSE_TERMS):
            term = rest.astype(BF16).astype(F32)
            rest = rest - term
            terms = jnp.where(lane == h * LSE_TERMS + t, term, terms)
    qx_ref[:, :width] = q_ref[...]
    qx_ref[:, width:] = terms.astype(BF16)
    finish(out)


def query_grad_kernel(n, core_ref, dattn_hbm, attn_hbm, probs_hbm, *refs):
    kv_hbm, (dq_ref, dattn_ref, attn_ref, probs_ref, kv_ref, sems) = refs[: n + 1], refs[n + 1 :]
    rows, width = attn_ref.shape
    fetch(
        (dattn_hbm, attn_hbm, probs_hbm, *split_parts(n, kv_hbm, rows)),
        (
            dattn_ref,
            attn_ref,
            probs_ref,
            *window_parts(core_ref, range(n - 1, -1, -1), kv_ref, rows),
        ),
        sems,
    )
    scale = HEAD_DIM ** (-0.5)
    for h in range(width // HEAD_DIM):
        cols = slice(h * HEAD_DIM, (h + 1) * HEAD_DIM)
        vcols = slice(width + h * HEAD_DIM, width + (h + 1) * HEAD_DIM)
        dattn = dattn_ref[:, cols]
        delta = jnp.sum(
            dattn.astype(F32) * attn_ref[:, cols].astype(F32), axis=-1, keepdims=True
        )
        dprobs = dot(dattn, kv_ref[:, vcols], NT)
        dscores = (probs_ref[h] * (dprobs - delta) * scale).astype(BF16)
        dq_ref[:, cols] = dot(dscores, kv_ref[:, cols]).astype(BF16)


def key_grad_kernel(n, core_ref, qseg_ref, kseg_ref, kv_hbm, qx_hbm, attn_hbm, *refs):
    dattn_hbm, refs = refs[: n + 1], refs[n + 1 :]
    dkey_ref, dvalue_ref, kv_ref, qx_ref, attn_ref, dattn_ref, sems = refs
    rows, width = dkey_ref.shape
    queries = 2 * rows * n
    fetch(
        (kv_hbm, qx_hbm, attn_hbm, *split_parts(n, dattn_hbm, rows)),
        (kv_ref, qx_ref, attn_ref, *window_parts(core_ref, range(n), dattn_ref, rows)),
        sems,
    )
    scale = HEAD_DIM ** (-0.5)
    place = lax.broadcasted_iota(jnp.int32, (queries, rows), 1) + core_ref[0] * rows
    allowed = (lax.broadcasted_iota(jnp.int32, (queries, rows), 0) >= place) & (
        qseg_ref[...] == kseg_ref[...]
    )
    for h in range(width // HEAD_DIM):
        cols = slice(h * HEAD_DIM, (h + 1) * HEAD_DIM)
        vcols = slice(width + h * HEAD_DIM, width + (h + 1) * HEAD_DIM)
        terms = qx_ref[:, width : width + HEAD_DIM].astype(F32)
        lse = terms[:, h * LSE_TERMS : h * LSE_TERMS + 1]
        for t in range(1, LSE_TERMS):
            lse = lse + terms[:, h * LSE_TERMS + t : h * LSE_TERMS + t + 1]
        query, dattn = qx_ref[:, cols], dattn_ref[:, cols]
        scores = dot(query, kv_ref[:, cols], NT) * scale
        probs = jnp.exp(jnp.where(allowed, scores - lse, -1e30))
        delta = jnp.sum(
            dattn.astype(F32) * attn_ref[:, cols].astype(F32), axis=-1, keepdims=True
        )
        dprobs = dot(dattn, kv_ref[:, vcols], NT)
        dscores = (probs * (dprobs - delta) * scale).astype(BF16)
        dkey_ref[:, cols] = dot(dscores, query, TN).astype(BF16)
        dvalue_ref[:, cols] = dot(probs.astype(BF16), dattn, TN).astype(BF16)


def loss_kernel(n, offsets, z_ref, *refs):
    terms_hbm, proj_hbm, refs = refs[:4], refs[4 : 4 + len(offsets)], refs[4 + len(offsets) :]
    out_ref, dpred_hbm, *terms_refs, dpred_ref = refs[:7]
    *proj_refs, sems = refs[7:]
    terms = begin(terms_hbm, terms_refs, sems)
    copies = begin(proj_hbm, proj_refs, sems, len(terms))
    finish(terms)
    first = 0
    for mine, other in (terms_refs[:2], terms_refs[2:]):
        diff = (mine[...].astype(F32) + other[...].astype(F32)).astype(BF16)
        dpred_ref[:, first : first + diff.shape[1]] = diff
        first += diff.shape[1]
    copies += begin([dpred_ref], [dpred_hbm], sems, len(terms) + len(copies))
    finish(copies[:-1])
    first = [0] * n
    for ref, by in zip(proj_refs, offsets, strict=True):
        size = ref.shape[0]
        z = lax.rem(z_ref[0] + by, n)
        out = dot(dpred_ref[...], ref[...], NT).astype(BF16)
        out_ref[z, :, first[by] : first[by] + size] = out
        first[by] += size
    finish(copies[-1:])


def proj_grad_kernel(n, attn_hbm, dpred_hbm, out_hbm, attn_ref, dpred_ref, out_ref, sems):
    rows = dpred_ref.shape[0] // n
    parts = [pl.ds(i * rows, rows) for i in range(n)]
    attn = begin([attn_hbm], [attn_ref], sems)
    dpred = begin([dpred_hbm.at[p] for p in parts], [dpred_ref.at[p] for p in parts], sems, 1)
    finish(attn)
    total = None
    for p, copy in zip(parts, dpred, strict=True):
        copy.wait()
        term = dot(attn_ref[p, :], dpred_ref[p, :], TN)
        total = term if total is None else total + term
    out_ref[...] = total.astype(BF16)
    fetch([out_ref], [out_hbm], sems)


def difference_kernel(n, z_ref, xh_ref, attn_hbm, proj_hbm, resid_hbm, teacher_hbm, sum_hbm, *refs):
    ring_refs, refs = refs[:n], refs[n:]
    attn_ref, proj_ref, resid_ref, teacher_ref, sum_ref, sems = refs
    rows = attn_ref.shape[0] // n
    split = sum_ref.shape[1]

    def at(r):
        return pl.ds(pl.multiple_of(lax.rem(z_ref[0] + r, n) * rows, rows), rows)

    own = [pl.ds(r * rows, rows) for r in range(n)]
    first = begin((attn_hbm, proj_hbm, resid_hbm), (attn_ref, proj_ref, resid_ref), sems)
    reads = begin(
        [teacher_hbm.at[at(r)] for r in range(n)], [teacher_ref.at[p] for p in own], sems, 3
    )
    finish(first)
    writes = []
    for r in range(n):
        reads[r].wait()
        out = dot(attn_ref[at(r), :], proj_ref[...]) - teacher_ref[own[r], :].astype(F32)
        if r == 0:
            resid = resid_ref[...].astype(F32)
            place = lax.broadcasted_iota(jnp.int32, out.shape, 0) // resid.shape[0]
            pair = jnp.concatenate([resid] * (rows // resid.shape[0]), axis=0)
            out = out - jnp.where(place == xh_ref[0], pair, 0.0)
        out = out.astype(BF16)
        sum_ref[own[r], :] = out[:, :split]
        writes += begin([sum_ref.at[own[r]]], [sum_hbm.at[at(r)]], sems, 3 + n + r)
        ring_refs[r][...] = out[:, split:]
    finish(writes)


def call(kernel, out_shape, in_smem, in_vmem, in_hbm, scratch, loose=()):
    space = pl.BlockSpec
    out_specs = jax.tree.map(
        lambda x: space(
            memory_space=pltpu.VMEM if isinstance(x, jax.ShapeDtypeStruct) else pltpu.HBM
        ),
        out_shape,
    )
    in_hbm = [
        x if i in loose else pltpu.with_memory_space_constraint(x, pltpu.HBM)
        for i, x in enumerate(in_hbm)
    ]
    return pl.pallas_call(
        kernel,
        out_shape=out_shape,
        out_specs=out_specs,
        in_specs=[space(memory_space=pltpu.SMEM)] * len(in_smem)
        + [space(memory_space=pltpu.VMEM)] * len(in_vmem)
        + [space(memory_space=pltpu.HBM)] * len(in_hbm),
        scratch_shapes=[pltpu.VMEM(s.shape, s.dtype) for s in scratch]
        + [pltpu.SemaphoreType.DMA((COPIES,))],
        compiler_params=pltpu.CompilerParams(vmem_limit_bytes=20 * 1024 * 1024),
    )(*in_smem, *in_vmem, *in_hbm)


def body(context, w_out, teacher_resid, queries, keys, values, segment_ids, proj):
    rows, width = queries.shape
    heads = width // HEAD_DIM
    n_sp, n_z, n_xh = lax.axis_size(SP), lax.axis_size("z"), lax.axis_size("xh")
    n_core = lax.axis_size("core")
    n_chip = n_sp // n_core
    near = min(-(-(SEGMENT_MAX - 1) // (n_core * rows)), n_chip - 1) + 1
    window = near * n_core * rows
    sp, core = lax.axis_index(SP), lax.axis_index("core")
    first_row, chip_row = sp * rows, (sp - core) * rows
    z, xh = lax.axis_index("z"), lax.axis_index("xh")
    core_scalar = core[None]

    def shift(array, by):
        by = by * n_core
        pairs = [(i, i + by) for i in range(n_sp) if 0 <= i + by < n_sp]
        return lax.ppermute(array, SP, pairs)

    def other_core(arrays):
        stacked = jnp.concatenate(arrays, axis=0)
        return lax.ppermute(stacked, "core", [(i, i ^ 1) for i in range(n_core)])

    def everywhere(array):
        copies = jnp.broadcast_to(array[None], (n_sp, *array.shape))
        return lax.all_to_all(copies, SP, 0, 0, tiled=True).reshape(-1, array.shape[1])

    def turn(array, by):
        return lax.ppermute(array, "z", [(i, (i + by) % n_z) for i in range(n_z)])

    def swap(array):
        return lax.ppermute(array, "xh", [(i, i ^ 1) for i in range(n_xh)])

    context_all = lax.all_gather(context, SP, axis=0, tiled=True)

    half = width // 2
    pieces, offsets = [proj], [0]

    def step(up, down):
        k = len(pieces) // 2 + 1
        offsets.extend([n_z - k, k])
        return turn(up, 1), turn(down, -1)

    key_value = jnp.concatenate([keys, values], axis=1)
    shifted = [shift(key_value, k) for k in range(1, near)]
    up, down = step(proj, proj)
    key_value, up, down = lax.optimization_barrier((key_value, up, down))
    pieces += [up, down]
    kv_parts = (key_value, *shifted, other_core([key_value, *shifted]))

    nobody = jnp.full((window - n_core * rows,), -1, jnp.int32)
    key_segments = lax.dynamic_slice_in_dim(
        jnp.concatenate([nobody, segment_ids]), chip_row, window, 0
    )
    query_segments = lax.dynamic_slice_in_dim(
        jnp.concatenate([segment_ids, nobody]), chip_row, window, 0
    )
    own_segments = lax.dynamic_slice_in_dim(segment_ids, first_row, rows, 0)
    block_type = jax.ShapeDtypeStruct((rows, width), BF16)
    window_type = jax.ShapeDtypeStruct((window, width), BF16)
    window_kv_type = jax.ShapeDtypeStruct((window, 2 * width), BF16)
    window_qx_type = jax.ShapeDtypeStruct((window, width + HEAD_DIM), BF16)
    probs_type = jax.ShapeDtypeStruct((heads, rows, window), F32)
    attn, probs, qx = call(
        functools.partial(forward_kernel, near),
        (
            block_type,
            pltpu.HBM(probs_type.shape, F32),
            jax.ShapeDtypeStruct((rows, width + HEAD_DIM), BF16),
        ),
        (core_scalar,),
        (own_segments[:, None], key_segments[None, :]),
        (queries, *kv_parts),
        (block_type, window_kv_type, probs_type),
    )
    attn_all = everywhere(attn)
    up, down = step(up, down)
    pieces += [up, down]
    up, down = step(up, down)
    teacher_part = dot(context_all, w_out).astype(BF16)
    teacher_part, qx, up, down = lax.optimization_barrier((teacher_part, qx, up, down))
    pieces += [up, down]

    def after(array):
        array = jnp.pad(array, ((0, window - n_core * rows), (0, 0)))
        return lax.dynamic_slice_in_dim(array, chip_row, window, 0)

    qx_after, attn_after = after(everywhere(qx)), after(attn_all)

    tokens, features = teacher_part.shape
    split = features * 3 // 4 // 128 * 128
    pair = n_xh * rows
    part, *ring = call(
        functools.partial(difference_kernel, n_z),
        (
            pltpu.HBM((tokens, split), BF16),
            *[jax.ShapeDtypeStruct((pair, features - split), BF16)] * n_z,
        ),
        (z[None], xh[None]),
        (),
        (attn_all, proj, teacher_resid, teacher_part),
        (attn_all, proj, teacher_resid, teacher_part, jax.ShapeDtypeStruct((tokens, split), BF16)),
    )
    part = lax.psum_scatter(part, "z", scatter_dimension=0, tiled=True)

    def plus(*arrays):
        return sum(x.astype(F32) for x in arrays).astype(BF16)

    right, left = turn(ring[n_z // 2], 1), turn(ring[n_z // 2 + 1], -1)
    for r in range(n_z // 2 - 1, 0, -1):
        right = turn(plus(ring[r], right), 1)
        if r > 1:
            left = turn(plus(ring[n_z - r + 1], left), -1)
    ring_sum = plus(ring[0], right, left)
    ring_other = swap(ring_sum)
    up, down = up[:half], down[half:]
    part, ring_other, qx_after, attn_after, up, down = lax.optimization_barrier(
        (part, ring_other, qx_after, attn_after, up, down)
    )
    part_other = swap(part)
    up, down = step(up, down)
    part_other, up, down = lax.optimization_barrier((part_other, up, down))
    pieces += [up, down]
    dattn_part, dpred = call(
        functools.partial(loss_kernel, n_z, offsets),
        (
            jax.ShapeDtypeStruct((n_z, pair, width), BF16),
            pltpu.HBM((pair, features), BF16),
        ),
        (z[None],),
        (),
        (part, part_other, ring_sum, ring_other, *pieces),
        (
            *(part, part_other, ring_sum, ring_other),
            jax.ShapeDtypeStruct((pair, features), BF16),
            *pieces,
        ),
        loose=(1, 2, 3, 4 + len(pieces) - 2, 4 + len(pieces) - 1),
    )
    dattn_parts = lax.all_to_all(dattn_part.reshape(n_sp, rows, width), SP, 0, 0, tiled=True)
    dattn = jnp.sum(dattn_parts.astype(F32), axis=0).astype(BF16)
    pairs = []
    for a in range(n_z):
        for x in range(n_xh):
            for b in range(n_z):
                for e in range(n_xh):
                    pairs.append(
                        (
                            (a * n_xh + x) * n_sp + b * n_xh + e,
                            (b * n_xh + x) * n_sp + a * n_xh + e,
                        )
                    )
    dattn = lax.ppermute(dattn, TP + SP, pairs)

    dpred_all = lax.all_gather(dpred, "z", axis=0, tiled=True)
    proj_grad = call(
        functools.partial(proj_grad_kernel, 4),
        pltpu.HBM(proj.shape, BF16),
        (),
        (),
        (attn_all, dpred_all),
        (attn_all, dpred_all, proj),
    )

    shifted = [shift(dattn, -k) for k in range(1, near)]
    query_grad = call(
        functools.partial(query_grad_kernel, near),
        block_type,
        (core_scalar,),
        (),
        (dattn, attn, probs, *kv_parts),
        (block_type, block_type, probs_type, window_kv_type),
        loose=(0,),
    )
    key_value, query_grad = lax.optimization_barrier((key_value, query_grad))
    key_grad, value_grad = call(
        functools.partial(key_grad_kernel, near),
        (block_type, block_type),
        (core_scalar,),
        (query_segments[:, None], own_segments[None, :]),
        (key_value, qx_after, attn_after, dattn, *shifted, other_core([dattn, *shifted])),
        (
            jax.ShapeDtypeStruct((rows, 2 * width), BF16),
            window_qx_type,
            window_type,
            window_type,
        ),
        loose=range(3, 5 + near),
    )
    return proj_grad, query_grad, key_grad, value_grad


def solution(mesh):
    fine = Mesh(mesh.devices.reshape(8, 2, 4, 2, 2), TP + SP)
    in_specs = (
        P(SP, TP),
        P(TP, SP),
        P(TP, SP),
        P(SP, TP),
        P(SP, TP),
        P(SP, TP),
        P(),
        P(TP, SP),
    )
    out_specs = (P(TP, SP), P(SP, TP), P(SP, TP), P(SP, TP))
    return jax.shard_map(body, mesh=fine, in_specs=in_specs, out_specs=out_specs, check_vma=False)
```

```python
import functools

import jax
import jax.numpy as jnp
from jax import lax
from jax.experimental import pallas as pl
from jax.experimental.pallas import tpu as pltpu
from jax.sharding import Mesh
from jax.sharding import PartitionSpec as P

HEAD_DIM = 128
SEGMENT_MAX = 1024
LSE_TERMS = 3
COPIES = 24
TP = ("z", "xh")
SP = ("y", "xl", "core")
F32 = jnp.float32
BF16 = jnp.bfloat16
NT = (((1,), (1,)), ((), ()))
TN = (((0,), (0,)), ((), ()))


def dot(a, b, dims=(((1,), (0,)), ((), ()))):
    return lax.dot_general(a, b, dims, preferred_element_type=F32)


def begin(sources, targets, sems, first=0):
    copies = [
        pltpu.make_async_copy(src, dst, sems.at[first + i])
        for i, (src, dst) in enumerate(zip(sources, targets, strict=True))
    ]
    for copy in copies:
        copy.start()
    return copies


def finish(copies):
    for copy in copies:
        copy.wait()


def fetch(sources, targets, sems):
    finish(begin(sources, targets, sems))


def window_parts(core_ref, chips, whole_ref, rows):
    mine, other = [], []
    for i in chips:
        mine.append(whole_ref.at[pl.ds(pl.multiple_of((2 * i + core_ref[0]) * rows, rows), rows)])
        other.append(
            whole_ref.at[pl.ds(pl.multiple_of((2 * i + 1 - core_ref[0]) * rows, rows), rows)]
        )
    return mine + other


def split_parts(n, refs, rows):
    return [*refs[:n], *(refs[n].at[pl.ds(i * rows, rows)] for i in range(n))]


def forward_kernel(n, core_ref, qseg_ref, kseg_ref, q_hbm, *refs):
    kv_hbm, refs = refs[: n + 1], refs[n + 1 :]
    attn_ref, probs_hbm, qx_ref, q_ref, kv_ref, probs_ref, sems = refs
    out = []
    rows, width = q_ref.shape
    keys = 2 * rows * n
    chips = range(n - 1, -1, -1)
    fetch(
        (q_hbm, *split_parts(n, kv_hbm, rows)),
        (q_ref, *window_parts(core_ref, chips, kv_ref, rows)),
        sems,
    )
    scale = HEAD_DIM ** (-0.5)
    first = keys - 2 * rows + core_ref[0] * rows
    place = lax.broadcasted_iota(jnp.int32, (rows, keys), 0) + first
    allowed = (place >= lax.broadcasted_iota(jnp.int32, (rows, keys), 1)) & (
        qseg_ref[...] == kseg_ref[...]
    )
    lane = lax.broadcasted_iota(jnp.int32, (rows, HEAD_DIM), 1)
    terms = jnp.zeros((rows, HEAD_DIM), F32)
    for h in range(width // HEAD_DIM):
        cols = slice(h * HEAD_DIM, (h + 1) * HEAD_DIM)
        vcols = slice(width + h * HEAD_DIM, width + (h + 1) * HEAD_DIM)
        scores = jnp.where(allowed, dot(q_ref[:, cols], kv_ref[:, cols], NT) * scale, -1e30)
        top = jnp.max(scores, axis=-1, keepdims=True)
        expo = jnp.exp(scores - top)
        total = jnp.sum(expo, axis=-1, keepdims=True)
        probs = expo / total
        probs_ref[h] = probs
        out += begin([probs_ref.at[h]], [probs_hbm.at[h]], sems, h)
        attn_ref[:, cols] = dot(probs.astype(BF16), kv_ref[:, vcols]).astype(BF16)
        rest = top + jnp.log(total)
        for t in range(LSE_TERMS):
            term = rest.astype(BF16).astype(F32)
            rest = rest - term
            terms = jnp.where(lane == h * LSE_TERMS + t, term, terms)
    qx_ref[:, :width] = q_ref[...]
    qx_ref[:, width:] = terms.astype(BF16)
    finish(out)


def query_grad_kernel(n, core_ref, dattn_hbm, attn_hbm, probs_hbm, *refs):
    kv_hbm, (dq_ref, dattn_ref, attn_ref, probs_ref, kv_ref, sems) = refs[: n + 1], refs[n + 1 :]
    rows, width = attn_ref.shape
    fetch(
        (dattn_hbm, attn_hbm, probs_hbm, *split_parts(n, kv_hbm, rows)),
        (
            dattn_ref,
            attn_ref,
            probs_ref,
            *window_parts(core_ref, range(n - 1, -1, -1), kv_ref, rows),
        ),
        sems,
    )
    scale = HEAD_DIM ** (-0.5)
    for h in range(width // HEAD_DIM):
        cols = slice(h * HEAD_DIM, (h + 1) * HEAD_DIM)
        vcols = slice(width + h * HEAD_DIM, width + (h + 1) * HEAD_DIM)
        dattn = dattn_ref[:, cols]
        delta = jnp.sum(
            dattn.astype(F32) * attn_ref[:, cols].astype(F32), axis=-1, keepdims=True
        )
        dprobs = dot(dattn, kv_ref[:, vcols], NT)
        dscores = (probs_ref[h] * (dprobs - delta) * scale).astype(BF16)
        dq_ref[:, cols] = dot(dscores, kv_ref[:, cols]).astype(BF16)


def key_grad_kernel(n, core_ref, qseg_ref, kseg_ref, kv_hbm, qx_hbm, attn_hbm, *refs):
    dattn_hbm, refs = refs[: n + 1], refs[n + 1 :]
    dkey_ref, dvalue_ref, kv_ref, qx_ref, attn_ref, dattn_ref, sems = refs
    rows, width = dkey_ref.shape
    queries = 2 * rows * n
    fetch(
        (kv_hbm, qx_hbm, attn_hbm, *split_parts(n, dattn_hbm, rows)),
        (kv_ref, qx_ref, attn_ref, *window_parts(core_ref, range(n), dattn_ref, rows)),
        sems,
    )
    scale = HEAD_DIM ** (-0.5)
    place = lax.broadcasted_iota(jnp.int32, (queries, rows), 1) + core_ref[0] * rows
    allowed = (lax.broadcasted_iota(jnp.int32, (queries, rows), 0) >= place) & (
        qseg_ref[...] == kseg_ref[...]
    )
    for h in range(width // HEAD_DIM):
        cols = slice(h * HEAD_DIM, (h + 1) * HEAD_DIM)
        vcols = slice(width + h * HEAD_DIM, width + (h + 1) * HEAD_DIM)
        terms = qx_ref[:, width : width + HEAD_DIM].astype(F32)
        lse = terms[:, h * LSE_TERMS : h * LSE_TERMS + 1]
        for t in range(1, LSE_TERMS):
            lse = lse + terms[:, h * LSE_TERMS + t : h * LSE_TERMS + t + 1]
        query, dattn = qx_ref[:, cols], dattn_ref[:, cols]
        scores = dot(query, kv_ref[:, cols], NT) * scale
        probs = jnp.exp(jnp.where(allowed, scores - lse, -1e30))
        delta = jnp.sum(
            dattn.astype(F32) * attn_ref[:, cols].astype(F32), axis=-1, keepdims=True
        )
        dprobs = dot(dattn, kv_ref[:, vcols], NT)
        dscores = (probs * (dprobs - delta) * scale).astype(BF16)
        dkey_ref[:, cols] = dot(dscores, query, TN).astype(BF16)
        dvalue_ref[:, cols] = dot(probs.astype(BF16), dattn, TN).astype(BF16)


def loss_kernel(*refs):
    n = (len(refs) - 3) // 4
    terms_hbm, dpred_hbm, terms_refs = refs[: 2 * n], refs[2 * n], refs[2 * n + 1 : 4 * n + 1]
    dpred_ref, sems = refs[4 * n + 1 :]
    terms = begin(terms_hbm, terms_refs, sems)
    first, out = 0, []
    for i in range(n):
        finish(terms[2 * i : 2 * i + 2])
        mine, other = terms_refs[2 * i : 2 * i + 2]
        here = pl.ds(first, mine.shape[1])
        dpred_ref[:, here] = (mine[...].astype(F32) + other[...].astype(F32)).astype(BF16)
        out += begin([dpred_ref.at[:, here]], [dpred_hbm.at[:, here]], sems, 2 * n + i)
        first += mine.shape[1]
    finish(out)


def dattn_kernel(n, offsets, z_ref, dpred_hbm, *refs):
    proj_hbm, (out_ref, dpred_ref, *proj_refs, sems) = refs[: len(offsets)], refs[len(offsets) :]
    fetch((dpred_hbm, *proj_hbm), (dpred_ref, *proj_refs), sems)
    first = [0] * n
    for ref, by in zip(proj_refs, offsets, strict=True):
        size = ref.shape[0]
        z = lax.rem(z_ref[0] + by, n)
        out = dot(dpred_ref[...], ref[...], NT).astype(BF16)
        out_ref[z, :, first[by] : first[by] + size] = out
        first[by] += size


def proj_grad_kernel(n, attn_hbm, dpred_hbm, out_hbm, attn_ref, dpred_ref, out_ref, sems):
    rows = dpred_ref.shape[0] // n
    parts = [pl.ds(i * rows, rows) for i in range(n)]
    attn = begin([attn_hbm], [attn_ref], sems)
    dpred = begin([dpred_hbm.at[p] for p in parts], [dpred_ref.at[p] for p in parts], sems, 1)
    finish(attn)
    total = None
    for p, copy in zip(parts, dpred, strict=True):
        copy.wait()
        term = dot(attn_ref[p, :], dpred_ref[p, :], TN)
        total = term if total is None else total + term
    out_ref[...] = total.astype(BF16)
    fetch([out_ref], [out_hbm], sems)


def difference_kernel(n, z_ref, xh_ref, attn_hbm, proj_hbm, resid_hbm, teacher_hbm, sum_hbm, *refs):
    ring_refs, refs = refs[:n], refs[n:]
    attn_ref, proj_ref, resid_ref, teacher_ref, sum_ref, sems = refs
    rows = attn_ref.shape[0] // n
    last = proj_ref.shape[1] - sum_ref.shape[1]

    def at(r):
        return pl.ds(pl.multiple_of(lax.rem(z_ref[0] + r, n) * rows, rows), rows)

    own = [pl.ds(r * rows, rows) for r in range(n)]
    first = begin((attn_hbm, proj_hbm, resid_hbm), (attn_ref, proj_ref, resid_ref), sems)
    reads = begin(
        [teacher_hbm.at[at(r)] for r in range(n)], [teacher_ref.at[p] for p in own], sems, 3
    )
    finish(first)
    writes = []
    for r in range(n):
        reads[r].wait()
        out = dot(attn_ref[at(r), :], proj_ref[...]) - teacher_ref[own[r], :].astype(F32)
        if r == 0:
            resid = resid_ref[...].astype(F32)
            place = lax.broadcasted_iota(jnp.int32, out.shape, 0) // resid.shape[0]
            pair = jnp.concatenate([resid] * (rows // resid.shape[0]), axis=0)
            out = out - jnp.where(place == xh_ref[0], pair, 0.0)
        out = out.astype(BF16)
        sum_ref[own[r], :] = out[:, last:]
        writes += begin([sum_ref.at[own[r]]], [sum_hbm.at[at(r)]], sems, 3 + n + r)
        ring_refs[r][...] = out[:, :last]
    finish(writes)


def call(kernel, out_shape, in_smem, in_vmem, in_hbm, scratch, loose=()):
    space = pl.BlockSpec
    out_specs = jax.tree.map(
        lambda x: space(
            memory_space=pltpu.VMEM if isinstance(x, jax.ShapeDtypeStruct) else pltpu.HBM
        ),
        out_shape,
    )
    in_hbm = [
        x if i in loose else pltpu.with_memory_space_constraint(x, pltpu.HBM)
        for i, x in enumerate(in_hbm)
    ]
    return pl.pallas_call(
        kernel,
        out_shape=out_shape,
        out_specs=out_specs,
        in_specs=[space(memory_space=pltpu.SMEM)] * len(in_smem)
        + [space(memory_space=pltpu.VMEM)] * len(in_vmem)
        + [space(memory_space=pltpu.HBM)] * len(in_hbm),
        scratch_shapes=[pltpu.VMEM(s.shape, s.dtype) for s in scratch]
        + [pltpu.SemaphoreType.DMA((COPIES,))],
        compiler_params=pltpu.CompilerParams(vmem_limit_bytes=14 * 1024 * 1024),
    )(*in_smem, *in_vmem, *in_hbm)


def body(context, w_out, teacher_resid, queries, keys, values, segment_ids, proj):
    rows, width = queries.shape
    heads = width // HEAD_DIM
    n_sp, n_z, n_xh = lax.axis_size(SP), lax.axis_size("z"), lax.axis_size("xh")
    n_core = lax.axis_size("core")
    n_chip = n_sp // n_core
    near = min(-(-(SEGMENT_MAX - 1) // (n_core * rows)), n_chip - 1) + 1
    window = near * n_core * rows
    sp, core = lax.axis_index(SP), lax.axis_index("core")
    first_row, chip_row = sp * rows, (sp - core) * rows
    z, xh = lax.axis_index("z"), lax.axis_index("xh")
    core_scalar = core[None]

    def shift(array, by):
        by = by * n_core
        pairs = [(i, i + by) for i in range(n_sp) if 0 <= i + by < n_sp]
        return lax.ppermute(array, SP, pairs)

    def other_core(arrays):
        stacked = jnp.concatenate(arrays, axis=0)
        return lax.ppermute(stacked, "core", [(i, i ^ 1) for i in range(n_core)])

    def everywhere(array):
        copies = jnp.broadcast_to(array[None], (n_sp, *array.shape))
        return lax.all_to_all(copies, SP, 0, 0, tiled=True).reshape(-1, array.shape[1])

    def turn(array, by):
        return lax.ppermute(array, "z", [(i, (i + by) % n_z) for i in range(n_z)])

    def swap(array):
        return lax.ppermute(array, "xh", [(i, i ^ 1) for i in range(n_xh)])

    context_all = lax.all_gather(context, SP, axis=0, tiled=True)

    half = width // 2
    pieces, offsets = [proj], [0]

    def step(up, down):
        k = len(pieces) // 2 + 1
        offsets.extend([n_z - k, k])
        return turn(up, 1), turn(down, -1)

    key_value = jnp.concatenate([keys, values], axis=1)
    shifted = [shift(key_value, k) for k in range(1, near)]
    up, down = step(proj, proj)
    key_value, up, down = lax.optimization_barrier((key_value, up, down))
    pieces += [up, down]
    kv_parts = (key_value, *shifted, other_core([key_value, *shifted]))

    nobody = jnp.full((window - n_core * rows,), -1, jnp.int32)
    key_segments = lax.dynamic_slice_in_dim(
        jnp.concatenate([nobody, segment_ids]), chip_row, window, 0
    )
    query_segments = lax.dynamic_slice_in_dim(
        jnp.concatenate([segment_ids, nobody]), chip_row, window, 0
    )
    own_segments = lax.dynamic_slice_in_dim(segment_ids, first_row, rows, 0)
    block_type = jax.ShapeDtypeStruct((rows, width), BF16)
    window_type = jax.ShapeDtypeStruct((window, width), BF16)
    window_kv_type = jax.ShapeDtypeStruct((window, 2 * width), BF16)
    window_qx_type = jax.ShapeDtypeStruct((window, width + HEAD_DIM), BF16)
    probs_type = jax.ShapeDtypeStruct((heads, rows, window), F32)
    attn, probs, qx = call(
        functools.partial(forward_kernel, near),
        (
            block_type,
            pltpu.HBM(probs_type.shape, F32),
            jax.ShapeDtypeStruct((rows, width + HEAD_DIM), BF16),
        ),
        (core_scalar,),
        (own_segments[:, None], key_segments[None, :]),
        (queries, *kv_parts),
        (block_type, window_kv_type, probs_type),
        loose=range(1, 2 + near),
    )
    attn_all = everywhere(attn)
    up, down = step(up, down)
    pieces += [up, down]
    up, down = step(up, down)
    teacher_part = dot(context_all, w_out).astype(BF16)
    teacher_part, qx, up, down = lax.optimization_barrier((teacher_part, qx, up, down))
    pieces += [up, down]

    def after(array):
        array = jnp.pad(array, ((0, window - n_core * rows), (0, 0)))
        return lax.dynamic_slice_in_dim(array, chip_row, window, 0)

    qx_after, attn_after = after(everywhere(qx)), after(attn_all)

    tokens, features = teacher_part.shape
    split = features * 3 // 4 // 128 * 128
    pair = n_xh * rows
    part, *ring = call(
        functools.partial(difference_kernel, n_z),
        (
            pltpu.HBM((tokens, split), BF16),
            *[jax.ShapeDtypeStruct((pair, features - split), BF16)] * n_z,
        ),
        (z[None], xh[None]),
        (),
        (attn_all, proj, teacher_resid, teacher_part),
        (attn_all, proj, teacher_resid, teacher_part, jax.ShapeDtypeStruct((tokens, split), BF16)),
    )
    part = lax.psum_scatter(part, "z", scatter_dimension=0, tiled=True)

    def plus(*arrays):
        return sum(x.astype(F32) for x in arrays).astype(BF16)

    right, left = turn(ring[n_z // 2], 1), turn(ring[n_z // 2 + 1], -1)
    for r in range(n_z // 2 - 1, 0, -1):
        right = turn(plus(ring[r], right), 1)
        if r > 1:
            left = turn(plus(ring[n_z - r + 1], left), -1)
    ring_sum = plus(ring[0], right, left)
    ring_other = swap(ring_sum)
    up, down = up[:half], down[half:]
    part, ring_other, qx_after, attn_after, up, down = lax.optimization_barrier(
        (part, ring_other, qx_after, attn_after, up, down)
    )
    part_other = swap(part)
    up, down = step(up, down)
    part_other, up, down = lax.optimization_barrier((part_other, up, down))
    pieces += [up, down]
    pair_type = jax.ShapeDtypeStruct((pair, features), BF16)
    dpred = call(
        loss_kernel,
        pltpu.HBM(pair_type.shape, BF16),
        (),
        (),
        (ring_sum, ring_other, part, part_other),
        (ring_sum, ring_other, part, part_other, pair_type),
        loose=(0, 1, 3),
    )
    dattn_part = call(
        functools.partial(dattn_kernel, n_z, offsets),
        jax.ShapeDtypeStruct((n_z, pair, width), BF16),
        (z[None],),
        (),
        (dpred, *pieces),
        (dpred, *pieces),
        loose=(len(pieces) - 1, len(pieces)),
    )
    dattn_parts = lax.all_to_all(dattn_part.reshape(n_sp, rows, width), SP, 0, 0, tiled=True)
    dattn = jnp.sum(dattn_parts.astype(F32), axis=0).astype(BF16)
    pairs = []
    for a in range(n_z):
        for x in range(n_xh):
            for b in range(n_z):
                for e in range(n_xh):
                    pairs.append(
                        (
                            (a * n_xh + x) * n_sp + b * n_xh + e,
                            (b * n_xh + x) * n_sp + a * n_xh + e,
                        )
                    )
    dattn = lax.ppermute(dattn, TP + SP, pairs)

    dpred_all = lax.all_gather(dpred, "z", axis=0, tiled=True)
    proj_grad = call(
        functools.partial(proj_grad_kernel, 4),
        pltpu.HBM(proj.shape, BF16),
        (),
        (),
        (attn_all, dpred_all),
        (attn_all, dpred_all, proj),
    )

    shifted = [shift(dattn, -k) for k in range(1, near)]
    query_grad = call(
        functools.partial(query_grad_kernel, near),
        block_type,
        (core_scalar,),
        (),
        (dattn, attn, probs, *kv_parts),
        (block_type, block_type, probs_type, window_kv_type),
        loose=(0,),
    )
    key_value, query_grad = lax.optimization_barrier((key_value, query_grad))
    key_grad, value_grad = call(
        functools.partial(key_grad_kernel, near),
        (block_type, block_type),
        (core_scalar,),
        (query_segments[:, None], own_segments[None, :]),
        (key_value, qx_after, attn_after, dattn, *shifted, other_core([dattn, *shifted])),
        (
            jax.ShapeDtypeStruct((rows, 2 * width), BF16),
            window_qx_type,
            window_type,
            window_type,
        ),
        loose=range(3, 5 + near),
    )
    return proj_grad, query_grad, key_grad, value_grad


def solution(mesh):
    fine = Mesh(mesh.devices.reshape(8, 2, 4, 2, 2), TP + SP)
    in_specs = (
        P(SP, TP),
        P(TP, SP),
        P(TP, SP),
        P(SP, TP),
        P(SP, TP),
        P(SP, TP),
        P(),
        P(TP, SP),
    )
    out_specs = (P(TP, SP), P(SP, TP), P(SP, TP), P(SP, TP))
    return jax.shard_map(body, mesh=fine, in_specs=in_specs, out_specs=out_specs, check_vma=False)
```

```python
import functools

import jax
import jax.numpy as jnp
from jax import lax
from jax.experimental import pallas as pl
from jax.experimental.pallas import tpu as pltpu
from jax.sharding import Mesh
from jax.sharding import PartitionSpec as P

HEAD_DIM = 128
SEGMENT_MAX = 1024
LSE_TERMS = 3
COPIES = 24
TP = ("z", "xh")
SP = ("y", "xl", "core")
F32 = jnp.float32
BF16 = jnp.bfloat16
NT = (((1,), (1,)), ((), ()))
TN = (((0,), (0,)), ((), ()))


def dot(a, b, dims=(((1,), (0,)), ((), ()))):
    return lax.dot_general(a, b, dims, preferred_element_type=F32)


def begin(sources, targets, sems, first=0):
    copies = [
        pltpu.make_async_copy(src, dst, sems.at[first + i])
        for i, (src, dst) in enumerate(zip(sources, targets, strict=True))
    ]
    for copy in copies:
        copy.start()
    return copies


def finish(copies):
    for copy in copies:
        copy.wait()


def fetch(sources, targets, sems):
    finish(begin(sources, targets, sems))


def window_parts(core_ref, chips, whole_ref, rows):
    mine, other = [], []
    for i in chips:
        mine.append(whole_ref.at[pl.ds(pl.multiple_of((2 * i + core_ref[0]) * rows, rows), rows)])
        other.append(
            whole_ref.at[pl.ds(pl.multiple_of((2 * i + 1 - core_ref[0]) * rows, rows), rows)]
        )
    return mine + other


def split_parts(n, refs, rows):
    return [*refs[:n], *(refs[n].at[pl.ds(i * rows, rows)] for i in range(n))]


def forward_kernel(n, core_ref, qseg_ref, kseg_ref, q_hbm, *refs):
    kv_hbm, refs = refs[: n + 1], refs[n + 1 :]
    attn_ref, probs_hbm, qx_ref, q_ref, kv_ref, probs_ref, sems = refs
    out = []
    rows, width = q_ref.shape
    keys = 2 * rows * n
    chips = range(n - 1, -1, -1)
    fetch(
        (q_hbm, *split_parts(n, kv_hbm, rows)),
        (q_ref, *window_parts(core_ref, chips, kv_ref, rows)),
        sems,
    )
    scale = HEAD_DIM ** (-0.5)
    first = keys - 2 * rows + core_ref[0] * rows
    place = lax.broadcasted_iota(jnp.int32, (rows, keys), 0) + first
    allowed = (place >= lax.broadcasted_iota(jnp.int32, (rows, keys), 1)) & (
        qseg_ref[...] == kseg_ref[...]
    )
    lane = lax.broadcasted_iota(jnp.int32, (rows, HEAD_DIM), 1)
    terms = jnp.zeros((rows, HEAD_DIM), F32)
    for h in range(width // HEAD_DIM):
        cols = slice(h * HEAD_DIM, (h + 1) * HEAD_DIM)
        vcols = slice(width + h * HEAD_DIM, width + (h + 1) * HEAD_DIM)
        scores = jnp.where(allowed, dot(q_ref[:, cols], kv_ref[:, cols], NT) * scale, -1e30)
        top = jnp.max(scores, axis=-1, keepdims=True)
        expo = jnp.exp(scores - top)
        total = jnp.sum(expo, axis=-1, keepdims=True)
        probs = expo / total
        probs_ref[h] = probs
        out += begin([probs_ref.at[h]], [probs_hbm.at[h]], sems, h)
        attn_ref[:, cols] = dot(probs.astype(BF16), kv_ref[:, vcols]).astype(BF16)
        rest = top + jnp.log(total)
        for t in range(LSE_TERMS):
            term = rest.astype(BF16).astype(F32)
            rest = rest - term
            terms = jnp.where(lane == h * LSE_TERMS + t, term, terms)
    qx_ref[:, :width] = q_ref[...]
    qx_ref[:, width:] = terms.astype(BF16)
    finish(out)


def query_grad_kernel(n, core_ref, dattn_hbm, attn_hbm, probs_hbm, *refs):
    kv_hbm, (dq_ref, dattn_ref, attn_ref, probs_ref, kv_ref, sems) = refs[: n + 1], refs[n + 1 :]
    rows, width = attn_ref.shape
    fetch(
        (dattn_hbm, attn_hbm, probs_hbm, *split_parts(n, kv_hbm, rows)),
        (
            dattn_ref,
            attn_ref,
            probs_ref,
            *window_parts(core_ref, range(n - 1, -1, -1), kv_ref, rows),
        ),
        sems,
    )
    scale = HEAD_DIM ** (-0.5)
    for h in range(width // HEAD_DIM):
        cols = slice(h * HEAD_DIM, (h + 1) * HEAD_DIM)
        vcols = slice(width + h * HEAD_DIM, width + (h + 1) * HEAD_DIM)
        dattn = dattn_ref[:, cols]
        delta = jnp.sum(
            dattn.astype(F32) * attn_ref[:, cols].astype(F32), axis=-1, keepdims=True
        )
        dprobs = dot(dattn, kv_ref[:, vcols], NT)
        dscores = (probs_ref[h] * (dprobs - delta) * scale).astype(BF16)
        dq_ref[:, cols] = dot(dscores, kv_ref[:, cols]).astype(BF16)


def key_grad_kernel(n, core_ref, qseg_ref, kseg_ref, kv_hbm, qx_hbm, attn_hbm, *refs):
    dattn_hbm, refs = refs[: n + 1], refs[n + 1 :]
    dkey_ref, dvalue_ref, kv_ref, qx_ref, attn_ref, dattn_ref, sems = refs
    rows, width = dkey_ref.shape
    queries = 2 * rows * n
    fetch(
        (kv_hbm, qx_hbm, attn_hbm, *split_parts(n, dattn_hbm, rows)),
        (kv_ref, qx_ref, attn_ref, *window_parts(core_ref, range(n), dattn_ref, rows)),
        sems,
    )
    scale = HEAD_DIM ** (-0.5)
    place = lax.broadcasted_iota(jnp.int32, (queries, rows), 1) + core_ref[0] * rows
    allowed = (lax.broadcasted_iota(jnp.int32, (queries, rows), 0) >= place) & (
        qseg_ref[...] == kseg_ref[...]
    )
    for h in range(width // HEAD_DIM):
        cols = slice(h * HEAD_DIM, (h + 1) * HEAD_DIM)
        vcols = slice(width + h * HEAD_DIM, width + (h + 1) * HEAD_DIM)
        terms = qx_ref[:, width : width + HEAD_DIM].astype(F32)
        lse = terms[:, h * LSE_TERMS : h * LSE_TERMS + 1]
        for t in range(1, LSE_TERMS):
            lse = lse + terms[:, h * LSE_TERMS + t : h * LSE_TERMS + t + 1]
        query, dattn = qx_ref[:, cols], dattn_ref[:, cols]
        scores = dot(query, kv_ref[:, cols], NT) * scale
        probs = jnp.exp(jnp.where(allowed, scores - lse, -1e30))
        delta = jnp.sum(
            dattn.astype(F32) * attn_ref[:, cols].astype(F32), axis=-1, keepdims=True
        )
        dprobs = dot(dattn, kv_ref[:, vcols], NT)
        dscores = (probs * (dprobs - delta) * scale).astype(BF16)
        dkey_ref[:, cols] = dot(dscores, query, TN).astype(BF16)
        dvalue_ref[:, cols] = dot(probs.astype(BF16), dattn, TN).astype(BF16)


def loss_kernel(*refs):
    n = (len(refs) - 3) // 4
    terms_hbm, dpred_hbm, terms_refs = refs[: 2 * n], refs[2 * n], refs[2 * n + 1 : 4 * n + 1]
    dpred_ref, sems = refs[4 * n + 1 :]
    terms = begin(terms_hbm, terms_refs, sems)
    first, out = 0, []
    for i in range(n):
        finish(terms[2 * i : 2 * i + 2])
        mine, other = terms_refs[2 * i : 2 * i + 2]
        here = pl.ds(first, mine.shape[1])
        dpred_ref[:, here] = (mine[...].astype(F32) + other[...].astype(F32)).astype(BF16)
        out += begin([dpred_ref.at[:, here]], [dpred_hbm.at[:, here]], sems, 2 * n + i)
        first += mine.shape[1]
    finish(out)


def dattn_kernel(n, offsets, z_ref, dpred_hbm, *refs):
    proj_hbm, (out_ref, dpred_ref, *proj_refs, sems) = refs[: len(offsets)], refs[len(offsets) :]
    fetch((dpred_hbm, *proj_hbm), (dpred_ref, *proj_refs), sems)
    first = [0] * n
    for ref, by in zip(proj_refs, offsets, strict=True):
        size = ref.shape[0]
        z = lax.rem(z_ref[0] + by, n)
        out = dot(dpred_ref[...], ref[...], NT).astype(BF16)
        out_ref[z, :, first[by] : first[by] + size] = out
        first[by] += size


def proj_grad_kernel(n, attn_hbm, dpred_hbm, out_hbm, attn_ref, dpred_ref, out_ref, sems):
    rows, columns = dpred_ref.shape[0] // n, dpred_ref.shape[1] // 2
    parts = [pl.ds(i * rows, rows) for i in range(n)]
    copies = begin([attn_hbm], [attn_ref], sems)
    copies += begin([dpred_hbm.at[p] for p in parts], [dpred_ref.at[p] for p in parts], sems, 1)
    finish(copies)
    writes = []
    for half in range(2):
        here = pl.ds(half * columns, columns)
        out_ref[:, here] = dot(attn_ref[...], dpred_ref[:, here], TN).astype(BF16)
        writes += begin([out_ref.at[:, here]], [out_hbm.at[:, here]], sems, 1 + n + half)
    finish(writes)


def difference_kernel(n, z_ref, xh_ref, attn_hbm, proj_hbm, resid_hbm, teacher_hbm, sum_hbm, *refs):
    ring_refs, refs = refs[:n], refs[n:]
    attn_ref, proj_ref, resid_ref, teacher_ref, sum_ref, sems = refs
    rows = attn_ref.shape[0] // n
    last = proj_ref.shape[1] - sum_ref.shape[1]

    def at(r):
        return pl.ds(pl.multiple_of(lax.rem(z_ref[0] + r, n) * rows, rows), rows)

    own = [pl.ds(r * rows, rows) for r in range(n)]
    first = begin((attn_hbm, proj_hbm, resid_hbm), (attn_ref, proj_ref, resid_ref), sems)
    reads = begin(
        [teacher_hbm.at[at(r)] for r in range(n)], [teacher_ref.at[p] for p in own], sems, 3
    )
    finish(first)
    writes = []
    for r in range(n):
        reads[r].wait()
        out = dot(attn_ref[at(r), :], proj_ref[...]) - teacher_ref[own[r], :].astype(F32)
        if r == 0:
            resid = resid_ref[...].astype(F32)
            place = lax.broadcasted_iota(jnp.int32, out.shape, 0) // resid.shape[0]
            pair = jnp.concatenate([resid] * (rows // resid.shape[0]), axis=0)
            out = out - jnp.where(place == xh_ref[0], pair, 0.0)
        out = out.astype(BF16)
        sum_ref[own[r], :] = out[:, last:]
        writes += begin([sum_ref.at[own[r]]], [sum_hbm.at[at(r)]], sems, 3 + n + r)
        ring_refs[r][...] = out[:, :last]
    finish(writes)


def call(kernel, out_shape, in_smem, in_vmem, in_hbm, scratch, loose=()):
    space = pl.BlockSpec
    out_specs = jax.tree.map(
        lambda x: space(
            memory_space=pltpu.VMEM if isinstance(x, jax.ShapeDtypeStruct) else pltpu.HBM
        ),
        out_shape,
    )
    in_hbm = [
        x if i in loose else pltpu.with_memory_space_constraint(x, pltpu.HBM)
        for i, x in enumerate(in_hbm)
    ]
    return pl.pallas_call(
        kernel,
        out_shape=out_shape,
        out_specs=out_specs,
        in_specs=[space(memory_space=pltpu.SMEM)] * len(in_smem)
        + [space(memory_space=pltpu.VMEM)] * len(in_vmem)
        + [space(memory_space=pltpu.HBM)] * len(in_hbm),
        scratch_shapes=[pltpu.VMEM(s.shape, s.dtype) for s in scratch]
        + [pltpu.SemaphoreType.DMA((COPIES,))],
        compiler_params=pltpu.CompilerParams(vmem_limit_bytes=14 * 1024 * 1024),
    )(*in_smem, *in_vmem, *in_hbm)


def body(context, w_out, teacher_resid, queries, keys, values, segment_ids, proj):
    rows, width = queries.shape
    heads = width // HEAD_DIM
    n_sp, n_z, n_xh = lax.axis_size(SP), lax.axis_size("z"), lax.axis_size("xh")
    n_core = lax.axis_size("core")
    n_chip = n_sp // n_core
    near = min(-(-(SEGMENT_MAX - 1) // (n_core * rows)), n_chip - 1) + 1
    window = near * n_core * rows
    sp, core = lax.axis_index(SP), lax.axis_index("core")
    first_row, chip_row = sp * rows, (sp - core) * rows
    z, xh = lax.axis_index("z"), lax.axis_index("xh")
    core_scalar = core[None]

    def shift(array, by):
        by = by * n_core
        pairs = [(i, i + by) for i in range(n_sp) if 0 <= i + by < n_sp]
        return lax.ppermute(array, SP, pairs)

    def other_core(arrays):
        stacked = jnp.concatenate(arrays, axis=0)
        return lax.ppermute(stacked, "core", [(i, i ^ 1) for i in range(n_core)])

    def everywhere(array):
        copies = jnp.broadcast_to(array[None], (n_sp, *array.shape))
        return lax.all_to_all(copies, SP, 0, 0, tiled=True).reshape(-1, array.shape[1])

    def turn(array, by):
        return lax.ppermute(array, "z", [(i, (i + by) % n_z) for i in range(n_z)])

    def swap(array):
        return lax.ppermute(array, "xh", [(i, i ^ 1) for i in range(n_xh)])

    context_all = lax.all_gather(context, SP, axis=0, tiled=True)

    half = width // 2
    pieces, offsets = [proj], [0]

    def step(up, down):
        k = len(pieces) // 2 + 1
        offsets.extend([n_z - k, k])
        return turn(up, 1), turn(down, -1)

    key_value = jnp.concatenate([keys, values], axis=1)
    shifted = [shift(key_value, k) for k in range(1, near)]
    up, down = step(proj, proj)
    key_value, up, down = lax.optimization_barrier((key_value, up, down))
    pieces += [up, down]
    kv_parts = (key_value, *shifted, other_core([key_value, *shifted]))

    nobody = jnp.full((window - n_core * rows,), -1, jnp.int32)
    key_segments = lax.dynamic_slice_in_dim(
        jnp.concatenate([nobody, segment_ids]), chip_row, window, 0
    )
    query_segments = lax.dynamic_slice_in_dim(
        jnp.concatenate([segment_ids, nobody]), chip_row, window, 0
    )
    own_segments = lax.dynamic_slice_in_dim(segment_ids, first_row, rows, 0)
    block_type = jax.ShapeDtypeStruct((rows, width), BF16)
    window_type = jax.ShapeDtypeStruct((window, width), BF16)
    window_kv_type = jax.ShapeDtypeStruct((window, 2 * width), BF16)
    window_qx_type = jax.ShapeDtypeStruct((window, width + HEAD_DIM), BF16)
    probs_type = jax.ShapeDtypeStruct((heads, rows, window), F32)
    attn, probs, qx = call(
        functools.partial(forward_kernel, near),
        (
            block_type,
            pltpu.HBM(probs_type.shape, F32),
            jax.ShapeDtypeStruct((rows, width + HEAD_DIM), BF16),
        ),
        (core_scalar,),
        (own_segments[:, None], key_segments[None, :]),
        (queries, *kv_parts),
        (block_type, window_kv_type, probs_type),
        loose=range(1, 2 + near),
    )
    attn_all = everywhere(attn)
    up, down = step(up, down)
    pieces += [up, down]
    up, down = step(up, down)
    teacher_part = dot(context_all, w_out).astype(BF16)
    teacher_part, qx, up, down = lax.optimization_barrier((teacher_part, qx, up, down))
    pieces += [up, down]

    def after(array):
        array = jnp.pad(array, ((0, window - n_core * rows), (0, 0)))
        return lax.dynamic_slice_in_dim(array, chip_row, window, 0)

    qx_after, attn_after = after(everywhere(qx)), after(attn_all)

    tokens, features = teacher_part.shape
    split = features * 3 // 4 // 128 * 128
    pair = n_xh * rows
    part, *ring = call(
        functools.partial(difference_kernel, n_z),
        (
            pltpu.HBM((tokens, split), BF16),
            *[jax.ShapeDtypeStruct((pair, features - split), BF16)] * n_z,
        ),
        (z[None], xh[None]),
        (),
        (attn_all, proj, teacher_resid, teacher_part),
        (attn_all, proj, teacher_resid, teacher_part, jax.ShapeDtypeStruct((tokens, split), BF16)),
    )
    part = lax.psum_scatter(part, "z", scatter_dimension=0, tiled=True)

    def plus(*arrays):
        return sum(x.astype(F32) for x in arrays).astype(BF16)

    right, left = turn(ring[n_z // 2], 1), turn(ring[n_z // 2 + 1], -1)
    for r in range(n_z // 2 - 1, 0, -1):
        right = turn(plus(ring[r], right), 1)
        if r > 1:
            left = turn(plus(ring[n_z - r + 1], left), -1)
    ring_sum = plus(ring[0], right, left)
    ring_other = swap(ring_sum)
    up, down = up[:half], down[half:]
    part, ring_other, qx_after, attn_after, up, down = lax.optimization_barrier(
        (part, ring_other, qx_after, attn_after, up, down)
    )
    part_other = swap(part)
    up, down = step(up, down)
    part_other, up, down = lax.optimization_barrier((part_other, up, down))
    pieces += [up, down]
    pair_type = jax.ShapeDtypeStruct((pair, features), BF16)
    dpred = call(
        loss_kernel,
        pltpu.HBM(pair_type.shape, BF16),
        (),
        (),
        (ring_sum, ring_other, part, part_other),
        (ring_sum, ring_other, part, part_other, pair_type),
        loose=(0, 1, 3),
    )
    dattn_part = call(
        functools.partial(dattn_kernel, n_z, offsets),
        jax.ShapeDtypeStruct((n_z, pair, width), BF16),
        (z[None],),
        (),
        (dpred, *pieces),
        (dpred, *pieces),
        loose=(len(pieces) - 1, len(pieces)),
    )
    dattn_parts = lax.all_to_all(dattn_part.reshape(n_sp, rows, width), SP, 0, 0, tiled=True)
    dattn = jnp.sum(dattn_parts.astype(F32), axis=0).astype(BF16)
    pairs = []
    for a in range(n_z):
        for x in range(n_xh):
            for b in range(n_z):
                for e in range(n_xh):
                    pairs.append(
                        (
                            (a * n_xh + x) * n_sp + b * n_xh + e,
                            (b * n_xh + x) * n_sp + a * n_xh + e,
                        )
                    )
    dattn = lax.ppermute(dattn, TP + SP, pairs)

    dpred_all = lax.all_gather(dpred, "z", axis=0, tiled=True)
    proj_grad = call(
        functools.partial(proj_grad_kernel, 4),
        pltpu.HBM(proj.shape, BF16),
        (),
        (),
        (attn_all, dpred_all),
        (attn_all, dpred_all, proj),
    )

    shifted = [shift(dattn, -k) for k in range(1, near)]
    query_grad = call(
        functools.partial(query_grad_kernel, near),
        block_type,
        (core_scalar,),
        (),
        (dattn, attn, probs, *kv_parts),
        (block_type, block_type, probs_type, window_kv_type),
        loose=(0,),
    )
    key_value, query_grad = lax.optimization_barrier((key_value, query_grad))
    key_grad, value_grad = call(
        functools.partial(key_grad_kernel, near),
        (block_type, block_type),
        (core_scalar,),
        (query_segments[:, None], own_segments[None, :]),
        (key_value, qx_after, attn_after, dattn, *shifted, other_core([dattn, *shifted])),
        (
            jax.ShapeDtypeStruct((rows, 2 * width), BF16),
            window_qx_type,
            window_type,
            window_type,
        ),
        loose=range(3, 5 + near),
    )
    return proj_grad, query_grad, key_grad, value_grad


def solution(mesh):
    fine = Mesh(mesh.devices.reshape(8, 2, 4, 2, 2), TP + SP)
    in_specs = (
        P(SP, TP),
        P(TP, SP),
        P(TP, SP),
        P(SP, TP),
        P(SP, TP),
        P(SP, TP),
        P(),
        P(TP, SP),
    )
    out_specs = (P(TP, SP), P(SP, TP), P(SP, TP), P(SP, TP))
    return jax.shard_map(body, mesh=fine, in_specs=in_specs, out_specs=out_specs, check_vma=False)
```

```python
import functools

import jax
import jax.numpy as jnp
from jax import lax
from jax.experimental import pallas as pl
from jax.experimental.pallas import tpu as pltpu
from jax.sharding import Mesh
from jax.sharding import PartitionSpec as P

HEAD_DIM = 128
SEGMENT_MAX = 1024
LSE_TERMS = 3
COPIES = 24
TP = ("z", "xh")
SP = ("y", "xl", "core")
F32 = jnp.float32
BF16 = jnp.bfloat16
NT = (((1,), (1,)), ((), ()))
TN = (((0,), (0,)), ((), ()))


def dot(a, b, dims=(((1,), (0,)), ((), ()))):
    return lax.dot_general(a, b, dims, preferred_element_type=F32)


def begin(sources, targets, sems, first=0):
    copies = [
        pltpu.make_async_copy(src, dst, sems.at[first + i])
        for i, (src, dst) in enumerate(zip(sources, targets, strict=True))
    ]
    for copy in copies:
        copy.start()
    return copies


def finish(copies):
    for copy in copies:
        copy.wait()


def fetch(sources, targets, sems):
    finish(begin(sources, targets, sems))


def window_parts(core_ref, chips, whole_ref, rows):
    mine, other = [], []
    for i in chips:
        mine.append(whole_ref.at[pl.ds(pl.multiple_of((2 * i + core_ref[0]) * rows, rows), rows)])
        other.append(
            whole_ref.at[pl.ds(pl.multiple_of((2 * i + 1 - core_ref[0]) * rows, rows), rows)]
        )
    return mine + other


def split_parts(n, refs, rows):
    return [*refs[:n], *(refs[n].at[pl.ds(i * rows, rows)] for i in range(n))]


def forward_kernel(n, core_ref, qseg_ref, kseg_ref, q_hbm, *refs):
    kv_hbm, refs = refs[: n + 1], refs[n + 1 :]
    attn_ref, probs_hbm, qx_ref, q_ref, kv_ref, probs_ref, sems = refs
    out = []
    rows, width = q_ref.shape
    keys = 2 * rows * n
    chips = range(n - 1, -1, -1)
    fetch(
        (q_hbm, *split_parts(n, kv_hbm, rows)),
        (q_ref, *window_parts(core_ref, chips, kv_ref, rows)),
        sems,
    )
    scale = HEAD_DIM ** (-0.5)
    first = keys - 2 * rows + core_ref[0] * rows
    place = lax.broadcasted_iota(jnp.int32, (rows, keys), 0) + first
    allowed = (place >= lax.broadcasted_iota(jnp.int32, (rows, keys), 1)) & (
        qseg_ref[...] == kseg_ref[...]
    )
    lane = lax.broadcasted_iota(jnp.int32, (rows, HEAD_DIM), 1)
    terms = jnp.zeros((rows, HEAD_DIM), F32)
    for h in range(width // HEAD_DIM):
        cols = slice(h * HEAD_DIM, (h + 1) * HEAD_DIM)
        vcols = slice(width + h * HEAD_DIM, width + (h + 1) * HEAD_DIM)
        scores = jnp.where(allowed, dot(q_ref[:, cols], kv_ref[:, cols], NT) * scale, -1e30)
        top = jnp.max(scores, axis=-1, keepdims=True)
        expo = jnp.exp(scores - top)
        total = jnp.sum(expo, axis=-1, keepdims=True)
        probs = expo / total
        probs_ref[h] = probs
        out += begin([probs_ref.at[h]], [probs_hbm.at[h]], sems, h)
        attn_ref[:, cols] = dot(probs.astype(BF16), kv_ref[:, vcols]).astype(BF16)
        rest = top + jnp.log(total)
        for t in range(LSE_TERMS):
            term = rest.astype(BF16).astype(F32)
            rest = rest - term
            terms = jnp.where(lane == h * LSE_TERMS + t, term, terms)
    qx_ref[:, :width] = q_ref[...]
    qx_ref[:, width:] = terms.astype(BF16)
    finish(out)


def query_grad_kernel(n, core_ref, dattn_hbm, attn_hbm, probs_hbm, *refs):
    kv_hbm, (dq_ref, dattn_ref, attn_ref, probs_ref, kv_ref, sems) = refs[: n + 1], refs[n + 1 :]
    rows, width = attn_ref.shape
    fetch(
        (dattn_hbm, attn_hbm, probs_hbm, *split_parts(n, kv_hbm, rows)),
        (
            dattn_ref,
            attn_ref,
            probs_ref,
            *window_parts(core_ref, range(n - 1, -1, -1), kv_ref, rows),
        ),
        sems,
    )
    scale = HEAD_DIM ** (-0.5)
    for h in range(width // HEAD_DIM):
        cols = slice(h * HEAD_DIM, (h + 1) * HEAD_DIM)
        vcols = slice(width + h * HEAD_DIM, width + (h + 1) * HEAD_DIM)
        dattn = dattn_ref[:, cols]
        delta = jnp.sum(
            dattn.astype(F32) * attn_ref[:, cols].astype(F32), axis=-1, keepdims=True
        )
        dprobs = dot(dattn, kv_ref[:, vcols], NT)
        dscores = (probs_ref[h] * (dprobs - delta) * scale).astype(BF16)
        dq_ref[:, cols] = dot(dscores, kv_ref[:, cols]).astype(BF16)


def key_grad_kernel(n, core_ref, qseg_ref, kseg_ref, kv_hbm, qx_hbm, attn_hbm, *refs):
    dattn_hbm, refs = refs[: n + 1], refs[n + 1 :]
    dkey_ref, dvalue_ref, kv_ref, qx_ref, attn_ref, dattn_ref, sems = refs
    rows, width = dkey_ref.shape
    queries = 2 * rows * n
    fetch(
        (kv_hbm, qx_hbm, attn_hbm, *split_parts(n, dattn_hbm, rows)),
        (kv_ref, qx_ref, attn_ref, *window_parts(core_ref, range(n), dattn_ref, rows)),
        sems,
    )
    scale = HEAD_DIM ** (-0.5)
    place = lax.broadcasted_iota(jnp.int32, (queries, rows), 1) + core_ref[0] * rows
    allowed = (lax.broadcasted_iota(jnp.int32, (queries, rows), 0) >= place) & (
        qseg_ref[...] == kseg_ref[...]
    )
    for h in range(width // HEAD_DIM):
        cols = slice(h * HEAD_DIM, (h + 1) * HEAD_DIM)
        vcols = slice(width + h * HEAD_DIM, width + (h + 1) * HEAD_DIM)
        terms = qx_ref[:, width : width + HEAD_DIM].astype(F32)
        lse = terms[:, h * LSE_TERMS : h * LSE_TERMS + 1]
        for t in range(1, LSE_TERMS):
            lse = lse + terms[:, h * LSE_TERMS + t : h * LSE_TERMS + t + 1]
        query, dattn = qx_ref[:, cols], dattn_ref[:, cols]
        scores = dot(query, kv_ref[:, cols], NT) * scale
        probs = jnp.exp(jnp.where(allowed, scores - lse, -1e30))
        delta = jnp.sum(
            dattn.astype(F32) * attn_ref[:, cols].astype(F32), axis=-1, keepdims=True
        )
        dprobs = dot(dattn, kv_ref[:, vcols], NT)
        dscores = (probs * (dprobs - delta) * scale).astype(BF16)
        dkey_ref[:, cols] = dot(dscores, query, TN).astype(BF16)
        dvalue_ref[:, cols] = dot(probs.astype(BF16), dattn, TN).astype(BF16)


def loss_kernel(*refs):
    n = (len(refs) - 3) // 4
    terms_hbm, dpred_hbm, terms_refs = refs[: 2 * n], refs[2 * n], refs[2 * n + 1 : 4 * n + 1]
    dpred_ref, sems = refs[4 * n + 1 :]
    terms = begin(terms_hbm, terms_refs, sems)
    first, out = 0, []
    for i in range(n):
        finish(terms[2 * i : 2 * i + 2])
        mine, other = terms_refs[2 * i : 2 * i + 2]
        here = pl.ds(first, mine.shape[1])
        dpred_ref[:, here] = (mine[...].astype(F32) + other[...].astype(F32)).astype(BF16)
        out += begin([dpred_ref.at[:, here]], [dpred_hbm.at[:, here]], sems, 2 * n + i)
        first += mine.shape[1]
    finish(out)


def dattn_kernel(n, offsets, z_ref, dpred_hbm, *refs):
    proj_hbm, (out_ref, dpred_ref, *proj_refs, sems) = refs[: len(offsets)], refs[len(offsets) :]
    fetch((dpred_hbm, *proj_hbm), (dpred_ref, *proj_refs), sems)
    first = [0] * n
    for ref, by in zip(proj_refs, offsets, strict=True):
        size = ref.shape[0]
        z = lax.rem(z_ref[0] + by, n)
        out = dot(dpred_ref[...], ref[...], NT).astype(BF16)
        out_ref[z, :, first[by] : first[by] + size] = out
        first[by] += size


def proj_grad_kernel(n, attn_hbm, dpred_hbm, out_hbm, attn_ref, dpred_ref, out_ref, sems):
    rows = dpred_ref.shape[0] // n
    parts = [pl.ds(i * rows, rows) for i in range(n)]
    attn = begin([attn_hbm], [attn_ref], sems)
    dpred = begin([dpred_hbm.at[p] for p in parts], [dpred_ref.at[p] for p in parts], sems, 1)
    finish(attn)
    total = None
    for p, copy in zip(parts, dpred, strict=True):
        copy.wait()
        term = dot(attn_ref[p, :], dpred_ref[p, :], TN)
        total = term if total is None else total + term
    out_ref[...] = total.astype(BF16)
    fetch([out_ref], [out_hbm], sems)


def difference_kernel(n, z_ref, xh_ref, attn_hbm, proj_hbm, resid_hbm, teacher_hbm, sum_hbm, *refs):
    ring_refs, refs = refs[:n], refs[n:]
    attn_ref, proj_ref, resid_ref, teacher_ref, sum_ref, sems = refs
    rows = attn_ref.shape[0] // n
    last = proj_ref.shape[1] - sum_ref.shape[1]

    def at(r):
        return pl.ds(pl.multiple_of(lax.rem(z_ref[0] + r, n) * rows, rows), rows)

    own = [pl.ds(r * rows, rows) for r in range(n)]
    first = begin((attn_hbm, proj_hbm, resid_hbm), (attn_ref, proj_ref, resid_ref), sems)
    reads = begin(
        [teacher_hbm.at[at(r)] for r in range(n)], [teacher_ref.at[p] for p in own], sems, 3
    )
    finish(first)
    writes = []
    for r in range(n):
        reads[r].wait()
        out = dot(attn_ref[at(r), :], proj_ref[...]) - teacher_ref[own[r], :].astype(F32)
        if r == 0:
            resid = resid_ref[...].astype(F32)
            place = lax.broadcasted_iota(jnp.int32, out.shape, 0) // resid.shape[0]
            pair = jnp.concatenate([resid] * (rows // resid.shape[0]), axis=0)
            out = out - jnp.where(place == xh_ref[0], pair, 0.0)
        out = out.astype(BF16)
        sum_ref[own[r], :] = out[:, last:]
        writes += begin([sum_ref.at[own[r]]], [sum_hbm.at[at(r)]], sems, 3 + n + r)
        ring_refs[r][...] = out[:, :last]
    finish(writes)


def call(kernel, out_shape, in_smem, in_vmem, in_hbm, scratch, loose=()):
    space = pl.BlockSpec
    out_specs = jax.tree.map(
        lambda x: space(
            memory_space=pltpu.VMEM if isinstance(x, jax.ShapeDtypeStruct) else pltpu.HBM
        ),
        out_shape,
    )
    in_hbm = [
        x if i in loose else pltpu.with_memory_space_constraint(x, pltpu.HBM)
        for i, x in enumerate(in_hbm)
    ]
    return pl.pallas_call(
        kernel,
        out_shape=out_shape,
        out_specs=out_specs,
        in_specs=[space(memory_space=pltpu.SMEM)] * len(in_smem)
        + [space(memory_space=pltpu.VMEM)] * len(in_vmem)
        + [space(memory_space=pltpu.HBM)] * len(in_hbm),
        scratch_shapes=[pltpu.VMEM(s.shape, s.dtype) for s in scratch]
        + [pltpu.SemaphoreType.DMA((COPIES,))],
        compiler_params=pltpu.CompilerParams(vmem_limit_bytes=14 * 1024 * 1024),
    )(*in_smem, *in_vmem, *in_hbm)


def body(context, w_out, teacher_resid, queries, keys, values, segment_ids, proj):
    rows, width = queries.shape
    heads = width // HEAD_DIM
    n_sp, n_z, n_xh = lax.axis_size(SP), lax.axis_size("z"), lax.axis_size("xh")
    n_core = lax.axis_size("core")
    n_chip = n_sp // n_core
    near = min(-(-(SEGMENT_MAX - 1) // (n_core * rows)), n_chip - 1) + 1
    window = near * n_core * rows
    sp, core = lax.axis_index(SP), lax.axis_index("core")
    first_row, chip_row = sp * rows, (sp - core) * rows
    z, xh = lax.axis_index("z"), lax.axis_index("xh")
    core_scalar = core[None]

    def shift(array, by):
        by = by * n_core
        pairs = [(i, i + by) for i in range(n_sp) if 0 <= i + by < n_sp]
        return lax.ppermute(array, SP, pairs)

    def other_core(arrays):
        stacked = jnp.concatenate(arrays, axis=0)
        return lax.ppermute(stacked, "core", [(i, i ^ 1) for i in range(n_core)])

    def everywhere(array):
        copies = jnp.broadcast_to(array[None], (n_sp, *array.shape))
        return lax.all_to_all(copies, SP, 0, 0, tiled=True).reshape(-1, array.shape[1])

    def turn(array, by):
        return lax.ppermute(array, "z", [(i, (i + by) % n_z) for i in range(n_z)])

    def swap(array):
        return lax.ppermute(array, "xh", [(i, i ^ 1) for i in range(n_xh)])

    context_all = lax.all_gather(context, SP, axis=0, tiled=True)

    half = width // 2
    pieces, offsets = [proj], [0]

    def step(up, down):
        k = len(pieces) // 2 + 1
        offsets.extend([n_z - k, k])
        return turn(up, 1), turn(down, -1)

    key_value = jnp.concatenate([keys, values], axis=1)
    shifted = [shift(key_value, k) for k in range(1, near)]
    up, down = step(proj, proj)
    key_value, up, down = lax.optimization_barrier((key_value, up, down))
    pieces += [up, down]
    kv_parts = (key_value, *shifted, other_core([key_value, *shifted]))

    nobody = jnp.full((window - n_core * rows,), -1, jnp.int32)
    key_segments = lax.dynamic_slice_in_dim(
        jnp.concatenate([nobody, segment_ids]), chip_row, window, 0
    )
    query_segments = lax.dynamic_slice_in_dim(
        jnp.concatenate([segment_ids, nobody]), chip_row, window, 0
    )
    own_segments = lax.dynamic_slice_in_dim(segment_ids, first_row, rows, 0)
    block_type = jax.ShapeDtypeStruct((rows, width), BF16)
    window_type = jax.ShapeDtypeStruct((window, width), BF16)
    window_kv_type = jax.ShapeDtypeStruct((window, 2 * width), BF16)
    window_qx_type = jax.ShapeDtypeStruct((window, width + HEAD_DIM), BF16)
    probs_type = jax.ShapeDtypeStruct((heads, rows, window), F32)
    attn, probs, qx = call(
        functools.partial(forward_kernel, near),
        (
            block_type,
            pltpu.HBM(probs_type.shape, F32),
            jax.ShapeDtypeStruct((rows, width + HEAD_DIM), BF16),
        ),
        (core_scalar,),
        (own_segments[:, None], key_segments[None, :]),
        (queries, *kv_parts),
        (block_type, window_kv_type, probs_type),
        loose=range(1, 2 + near),
    )
    attn_all = everywhere(attn)
    up, down = step(up, down)
    pieces += [up, down]
    up, down = step(up, down)
    teacher_part = dot(context_all, w_out).astype(BF16)
    teacher_part, qx, up, down = lax.optimization_barrier((teacher_part, qx, up, down))
    pieces += [up, down]

    def after(array):
        array = jnp.pad(array, ((0, window - n_core * rows), (0, 0)))
        return lax.dynamic_slice_in_dim(array, chip_row, window, 0)

    qx_after, attn_after = after(everywhere(qx)), after(attn_all)

    tokens, features = teacher_part.shape
    split = features * 3 // 4 // 128 * 128
    pair = n_xh * rows
    part, *ring = call(
        functools.partial(difference_kernel, n_z),
        (
            pltpu.HBM((tokens, split), BF16),
            *[jax.ShapeDtypeStruct((pair, features - split), BF16)] * n_z,
        ),
        (z[None], xh[None]),
        (),
        (attn_all, proj, teacher_resid, teacher_part),
        (attn_all, proj, teacher_resid, teacher_part, jax.ShapeDtypeStruct((tokens, split), BF16)),
        loose=(0,),
    )
    part = lax.psum_scatter(part, "z", scatter_dimension=0, tiled=True)

    def plus(*arrays):
        return sum(x.astype(F32) for x in arrays).astype(BF16)

    right, left = turn(ring[n_z // 2], 1), turn(ring[n_z // 2 + 1], -1)
    for r in range(n_z // 2 - 1, 0, -1):
        right = turn(plus(ring[r], right), 1)
        if r > 1:
            left = turn(plus(ring[n_z - r + 1], left), -1)
    ring_sum = plus(ring[0], right, left)
    ring_other = swap(ring_sum)
    up, down = up[:half], down[half:]
    part, ring_other, qx_after, attn_after, up, down = lax.optimization_barrier(
        (part, ring_other, qx_after, attn_after, up, down)
    )
    part_other = swap(part)
    up, down = step(up, down)
    part_other, up, down = lax.optimization_barrier((part_other, up, down))
    pieces += [up, down]
    pair_type = jax.ShapeDtypeStruct((pair, features), BF16)
    dpred = call(
        loss_kernel,
        pltpu.HBM(pair_type.shape, BF16),
        (),
        (),
        (ring_sum, ring_other, part, part_other),
        (ring_sum, ring_other, part, part_other, pair_type),
        loose=(0, 1, 3),
    )
    dattn_part = call(
        functools.partial(dattn_kernel, n_z, offsets),
        jax.ShapeDtypeStruct((n_z, pair, width), BF16),
        (z[None],),
        (),
        (dpred, *pieces),
        (dpred, *pieces),
        loose=(len(pieces) - 1, len(pieces)),
    )
    dattn_parts = lax.all_to_all(dattn_part.reshape(n_sp, rows, width), SP, 0, 0, tiled=True)
    dattn = jnp.sum(dattn_parts.astype(F32), axis=0).astype(BF16)
    pairs = []
    for a in range(n_z):
        for x in range(n_xh):
            for b in range(n_z):
                for e in range(n_xh):
                    pairs.append(
                        (
                            (a * n_xh + x) * n_sp + b * n_xh + e,
                            (b * n_xh + x) * n_sp + a * n_xh + e,
                        )
                    )
    dattn = lax.ppermute(dattn, TP + SP, pairs)

    dpred_all = lax.all_gather(dpred, "z", axis=0, tiled=True)
    proj_grad = call(
        functools.partial(proj_grad_kernel, 4),
        pltpu.HBM(proj.shape, BF16),
        (),
        (),
        (attn_all, dpred_all),
        (attn_all, dpred_all, proj),
    )

    shifted = [shift(dattn, -k) for k in range(1, near)]
    query_grad = call(
        functools.partial(query_grad_kernel, near),
        block_type,
        (core_scalar,),
        (),
        (dattn, attn, probs, *kv_parts),
        (block_type, block_type, probs_type, window_kv_type),
        loose=(0,),
    )
    key_value, query_grad = lax.optimization_barrier((key_value, query_grad))
    key_grad, value_grad = call(
        functools.partial(key_grad_kernel, near),
        (block_type, block_type),
        (core_scalar,),
        (query_segments[:, None], own_segments[None, :]),
        (key_value, qx_after, attn_after, dattn, *shifted, other_core([dattn, *shifted])),
        (
            jax.ShapeDtypeStruct((rows, 2 * width), BF16),
            window_qx_type,
            window_type,
            window_type,
        ),
        loose=range(3, 5 + near),
    )
    return proj_grad, query_grad, key_grad, value_grad


def solution(mesh):
    fine = Mesh(mesh.devices.reshape(8, 2, 4, 2, 2), TP + SP)
    in_specs = (
        P(SP, TP),
        P(TP, SP),
        P(TP, SP),
        P(SP, TP),
        P(SP, TP),
        P(SP, TP),
        P(),
        P(TP, SP),
    )
    out_specs = (P(TP, SP), P(SP, TP), P(SP, TP), P(SP, TP))
    return jax.shard_map(body, mesh=fine, in_specs=in_specs, out_specs=out_specs, check_vma=False)
```
